32 devices in a mesh: elem: 16 (over z, x, core), band: 2 (over y).
Axes of the slice: x: 2, y: 2, z: 4, core: 2. Of those that a mesh axis runs over, the one named last changes fastest.
Arguments:
- start_bands: bfloat16 [96, 256, 1024], P('elem', None, 'band'), may hold values from -6 to 6
- blocks: bfloat16 [96, 5, 256, 256], P('elem'), may hold values from -0.125 to 0.125
- neighbours: int32 [96, 5], P('elem'), may hold values from 0 to 95, as said below
- band_order: int32 [1024], replicated, may hold values from 0 to 1023, each once
- rotation: bfloat16 [1024, 1024], P('elem', 'band'), may hold values from -0.1875 to 0.1875
Outputs:
- final_bands: bfloat16 [96, 256, 1024], P('elem', None, 'band')
The draws below stay inside these ranges and needn't reach their ends.
Inputs may be any that keep to these rules, and one draw needn't show every extreme that they name: `neighbours`: the elements form a periodic grid of 32 columns of 3 elements; column c holds the ids c * 3 to c * 3 + 2 in a drawn order. Row e lists e, the element at the same place in the previous column, the one in the next column, then the previous and the next element within e's column, periodically, in that order. `band_order`: A permutation of the band numbers.
All inputs are finite; a program needn't handle non-finite values.
Results may differ from the reference program's by a relative error of at most 0.01.
Values may be sent and summed in bfloat16 or wider, within the bound.
No kernel may reach another device: no remote copies, remote signals or barrier semaphores. Data moves between devices by JAX's collectives and lax.ppermute only.
A program may use at most 64 MiB of HBM per device.

```python
import jax
import jax.numpy as jnp
from jax import lax

NB = 256
M = 1024
GY = 3
NGX = 32
ELEMS = 96


def draw_neighbours(key, part):
    column_keys = jax.random.split(jax.random.fold_in(key, 71), NGX)
    placing = jax.vmap(lambda single_key: jax.random.permutation(single_key, GY))(column_keys).astype(jnp.int32)
    columns = jnp.arange(NGX, dtype=jnp.int32)[:, None] * GY
    id_grid = columns + placing
    previous_col = jnp.roll(id_grid, 1, axis=0)
    next_col = jnp.roll(id_grid, -1, axis=0)
    previous_row = jnp.roll(id_grid, 1, axis=1)
    next_row = jnp.roll(id_grid, -1, axis=1)
    links = jnp.stack([id_grid, previous_col, next_col, previous_row, next_row], axis=-1).reshape(NGX * GY, 5)
    result = jnp.zeros((NGX * GY, 5), jnp.int32)
    return result.at[id_grid.reshape(-1)].set(links)


def shard_levels(own_key, shape, cuts, smallest, largest):
    factor_of, own = 1.0, jax.random.fold_in(own_key, 6)
    for dim, parts in cuts:
        draws = jnp.exp(jax.random.uniform(jax.random.fold_in(own, dim), (parts,), jnp.float32, smallest / len(cuts), largest / len(cuts)))
        factor_of = factor_of * jnp.repeat(draws, shape[dim] // parts).reshape([-1 if axis == dim else 1 for axis in range(len(shape))])
    return factor_of


def scatter_about(stream_key, dims, spread, limit, cuts=(), held_as=jnp.bfloat16):
    values = jax.random.normal(stream_key, dims, jnp.float32) * spread
    if len(cuts) > 0:
        values = shard_levels(stream_key, dims, cuts, -0.22, 0.18) * values
    return jnp.clip(values, min=-limit, max=limit).astype(held_as)


def setup_inputs(seed: int = 0) -> dict:
    streams_of = jax.random.split(jax.random.key(seed), 6)
    start_bands = scatter_about(streams_of[0], (ELEMS, NB, M), 1.0, 6.0, ((0, 16), (2, 2)))
    blocks = scatter_about(streams_of[1], (ELEMS, 5, NB, NB), (10 * NB) ** -0.5, 0.125, ((0, 16),))
    neighbours = draw_neighbours(jax.random.fold_in(streams_of[5], 71), 0)
    band_order = jax.random.permutation(streams_of[3], M).astype(jnp.int32)
    rotation = scatter_about(streams_of[4], (M, M), M ** -0.5, 0.1875, ((0, 16), (1, 2)))
    return {"start_bands": start_bands, "blocks": blocks, "neighbours": neighbours, "band_order": band_order, "rotation": rotation}


def apply_blocks(current, blocks, neighbours):
    def single(args):
        element_blocks, element_links = args
        picked = current[element_links]
        left = element_blocks.transpose(1, 0, 2).reshape(NB, 5 * NB)
        return jnp.dot(left, picked.reshape(5 * NB, M), preferred_element_type=jnp.float32)
    return lax.map(single, (blocks, neighbours))


def chebyshev(initial, blocks, neighbours):
    first_term = apply_blocks(initial, blocks, neighbours).astype(jnp.bfloat16)
    second_term = (2.0 * apply_blocks(first_term, blocks, neighbours) - initial.astype(jnp.float32)).astype(jnp.bfloat16)
    third_term = (2.0 * apply_blocks(second_term, blocks, neighbours) - first_term.astype(jnp.float32)).astype(jnp.bfloat16)
    return third_term


def reference(start_bands, blocks, neighbours, band_order, rotation):
    filtered = chebyshev(start_bands, blocks, neighbours)
    permuted = filtered[:, :, band_order].reshape(ELEMS * NB, M)
    rotated = jnp.dot(permuted, rotation, preferred_element_type=jnp.float32).astype(jnp.bfloat16)
    rotated = rotated.reshape(ELEMS, NB, M)
    return chebyshev(rotated, blocks, neighbours)
```

```python
import functools

import jax
import jax.numpy as jnp
from jax import lax
from jax.experimental import pallas as pl
from jax.experimental.pallas import tpu as pltpu
from jax.sharding import PartitionSpec as P

GY = 3
CHUNK = 256
MIB = 1024 * 1024


def step_kernel(first, last, column, *refs):
    refs = list(refs)
    odd_ref, links_ref, blocks_ref, far_outer, outer, inner, far_inner = refs[:7]
    refs = refs[7:]
    before = None
    if not first:
        before, refs = refs[:2], refs[2:]
    if last and column > 0:
        refs = refs[1:]
    if last:
        out_ref, held, arrived, made, left = refs
    else:
        new_outer, new_inner, held, arrived = refs
    odd = odd_ref[0]
    rows, copies = [], []
    for k in range(2 * GY):
        row = odd * GY + k if k < GY else (1 - odd) * GY + (k - GY)
        copy = pltpu.make_async_copy(blocks_ref.at[row], held.at[k], arrived.at[k])
        copy.start()
        rows.append(row)
        copies.append(copy)
    sent = []
    for k in range(2 * GY):
        row = rows[k]
        own, near, far = (outer, inner, far_outer) if k < GY else (inner, outer, far_inner)
        far_side = 1 + odd if k < GY else 2 - odd
        near_side = 3 - far_side

        def slot(side):
            return lax.rem(links_ref[row, side], GY)

        copies[k].wait()
        total = jnp.dot(held[k, 0], own[slot(0)], preferred_element_type=jnp.float32)
        total += jnp.dot(held[k, 3], own[slot(3)], preferred_element_type=jnp.float32)
        total += jnp.dot(held[k, 4], own[slot(4)], preferred_element_type=jnp.float32)
        total += jnp.dot(held[k, near_side], near[slot(near_side)], preferred_element_type=jnp.float32)
        total += jnp.dot(held[k, far_side], far[slot(far_side)], preferred_element_type=jnp.float32)
        if not first:
            total = 2.0 * total - before[k // GY][k % GY].astype(jnp.float32)
        if last:
            made[k] = total.astype(jnp.bfloat16)
            width = made.shape[2]
            copy = pltpu.make_async_copy(
                made.at[k], out_ref.at[row, :, pl.ds(column, width)], left.at[k]
            )
            copy.start()
            sent.append(copy)
        else:
            target = new_outer if k < GY else new_inner
            target[k % GY] = total.astype(jnp.bfloat16)
    for copy in sent:
        copy.wait()


def apply_step(odd, links, blocks, halos, current, before, out=None, column=0, out_shape=None):
    basis, width = current[0].shape[1:]
    last = out_shape is not None
    smem = pl.BlockSpec(memory_space=pltpu.SMEM)
    vmem = pl.BlockSpec(memory_space=pltpu.VMEM)
    anywhere = pl.BlockSpec(memory_space=pl.ANY)
    operands = [odd, links, blocks, halos[0], current[0], current[1], halos[1]]
    specs = [smem, smem, anywhere] + [vmem] * 4
    if before is not None:
        operands += list(before)
        specs += [vmem] * 2
    aliases = {}
    scratch = [
        pltpu.VMEM((2 * GY,) + blocks.shape[1:], blocks.dtype),
        pltpu.SemaphoreType.DMA((2 * GY,)),
    ]
    if last:
        if out is not None:
            aliases = {len(operands): 0}
            operands.append(out)
            specs.append(anywhere)
        shapes = jax.ShapeDtypeStruct(out_shape, jnp.bfloat16)
        out_specs = anywhere
        scratch += [
            pltpu.VMEM((2 * GY, basis, width), jnp.bfloat16),
            pltpu.SemaphoreType.DMA((2 * GY,)),
        ]
    else:
        shapes = [jax.ShapeDtypeStruct((GY, basis, width), jnp.bfloat16)] * 2
        out_specs = [vmem, vmem]
    flops = 2 * 2 * GY * blocks.shape[1] * basis * basis * width
    moved = 2 * blocks.size + 2 * 10 * GY * basis * width
    return pl.pallas_call(
        functools.partial(step_kernel, before is None, last, column),
        out_shape=shapes,
        in_specs=specs,
        out_specs=out_specs,
        scratch_shapes=scratch,
        input_output_aliases=aliases,
        compiler_params=pltpu.CompilerParams(vmem_limit_bytes=24 * MIB),
        cost_estimate=pl.CostEstimate(flops=flops, bytes_accessed=moved, transcendentals=0),
    )(*operands)


def rotate_kernel(count, *refs):
    pieces, matrix, outs = refs[:count], refs[count], refs[count + 1 :]
    for k in range(GY):
        row = 0
        total = None
        for piece in pieces:
            width = piece.shape[2]
            part = jnp.dot(piece[k], matrix[row : row + width, :], preferred_element_type=jnp.float32)
            total = part if total is None else total + part
            row += width
        column = 0
        for out in outs:
            width = out.shape[2]
            out[k] = total[:, column : column + width].astype(jnp.bfloat16)
            column += width


def rotate(pieces, matrix, widths):
    basis = pieces[0].shape[1]
    vmem = pl.BlockSpec(memory_space=pltpu.VMEM)
    flops = 2 * GY * basis * matrix.shape[0] * matrix.shape[1]
    moved = 2 * (matrix.size + GY * basis * (matrix.shape[0] + matrix.shape[1]))
    return pl.pallas_call(
        functools.partial(rotate_kernel, len(pieces)),
        out_shape=[jax.ShapeDtypeStruct((GY, basis, width), jnp.bfloat16) for width in widths],
        in_specs=[vmem] * (len(pieces) + 1),
        out_specs=[vmem] * len(widths),
        compiler_params=pltpu.CompilerParams(vmem_limit_bytes=24 * MIB),
        cost_estimate=pl.CostEstimate(flops=flops, bytes_accessed=moved, transcendentals=0),
    )(*pieces, matrix)


def exchange(array, axis, partner):
    return lax.ppermute(array, axis, [(i, partner(i)) for i in range(lax.axis_size(axis))])


def gathered_rotation(rotation, band_order):
    elems, bands = lax.axis_size("elem"), lax.axis_size("band")
    me = lax.axis_index("elem")
    bits = [1 << b for b in range(elems.bit_length() - 1)]
    bits = bits[1:] + bits[:1]
    owners = [0]
    rows = rotation
    for bit in bits:
        rows = jnp.concatenate([rows, exchange(rows, "elem", lambda i: i ^ bit)], axis=0)
        owners = owners + [owner ^ bit for owner in owners]
    share = rotation.shape[0]
    order = band_order.reshape(elems, share)[jnp.bitwise_xor(me, jnp.array(owners))].reshape(-1)
    total = order.shape[0]
    width = total // bands
    place = lax.iota(jnp.int32, total)
    band = jnp.bitwise_xor(place // width, lax.axis_index("band")) * width + place % width
    choice = (band[:, None] == order[None, :]).astype(jnp.bfloat16)
    return jnp.dot(choice, rows, preferred_element_type=jnp.float32).astype(jnp.bfloat16)


def body(start_bands, blocks, neighbours, band_order, rotation):
    elem_count, basis, width = start_bands.shape
    assert elem_count == 2 * GY
    elems, bands = lax.axis_size("elem"), lax.axis_size("band")
    odd = lax.axis_index("elem") % 2
    odd_flag = odd.astype(jnp.int32).reshape(1)
    chunk = min(CHUNK, width)
    starts = list(range(0, width, chunk))
    widths = [chunk] * len(starts)

    def cross(array):
        return exchange(array, "elem", lambda i: (i - 1) % elems if i % 2 == 0 else (i + 1) % elems)

    def intra(array):
        return exchange(array, "elem", lambda i: i ^ 1)

    def step(current, before, **output):
        halos = (cross(current[0]), intra(current[1]))
        return apply_step(odd_flag, neighbours, blocks, halos, current, before, **output)

    matrix = gathered_rotation(rotation, band_order)

    state = []
    for column in starts:
        part = lax.slice_in_dim(start_bands, column, column + chunk, axis=2)
        state.append(
            (
                lax.dynamic_slice_in_dim(part, odd * GY, GY, axis=0),
                lax.dynamic_slice_in_dim(part, (1 - odd) * GY, GY, axis=0),
            )
        )
    before = [None] * len(starts)
    for _ in range(3):
        for c in range(len(starts)):
            new = step(state[c], before[c])
            before[c], state[c] = state[c], tuple(new)

    rotated = []
    for side in range(2):
        own = [state[c][side] for c in range(len(starts))]
        pieces = list(own)
        for shift in range(1, bands):
            pieces += [exchange(piece, "band", lambda i: i ^ shift) for piece in own]
        rotated.append(rotate(pieces, matrix, widths))
    state = [(rotated[0][c], rotated[1][c]) for c in range(len(starts))]

    before = [None] * len(starts)
    for _ in range(2):
        for c in range(len(starts)):
            new = step(state[c], before[c])
            before[c], state[c] = state[c], tuple(new)
    out = None
    for c in range(len(starts)):
        out = step(state[c], before[c], out=out, column=starts[c], out_shape=start_bands.shape)
    return out


def solution(mesh):
    return jax.shard_map(
        body,
        mesh=mesh,
        in_specs=(
            P("elem", None, "band"),
            P("elem", None, None, None),
            P("elem", None),
            P(),
            P("elem", "band"),
        ),
        out_specs=P("elem", None, "band"),
        check_vma=False,
    )
```

```python
import functools

import jax
import jax.numpy as jnp
from jax import lax
from jax.experimental import pallas as pl
from jax.experimental.pallas import tpu as pltpu
from jax.sharding import PartitionSpec as P

GY = 3
CHUNK = 256
MIB = 1024 * 1024


def step_kernel(first, last, column, *refs):
    refs = list(refs)
    odd_ref, links_ref, blocks_ref, far_outer, outer, inner, far_inner = refs[:7]
    refs = refs[7:]
    before = None
    if not first:
        before, refs = refs[:2], refs[2:]
    if last and column > 0:
        refs = refs[1:]
    if last:
        out_ref, made, left = refs
    else:
        new_outer, new_inner = refs
    odd = odd_ref[0]
    sent = []
    for k in range(2 * GY):
        row = odd * GY + k if k < GY else (1 - odd) * GY + (k - GY)
        own, near, far = (outer, inner, far_outer) if k < GY else (inner, outer, far_inner)
        far_side = 1 + odd if k < GY else 2 - odd
        near_side = 3 - far_side

        def slot(side):
            return lax.rem(links_ref[row, side], GY)

        total = jnp.dot(blocks_ref[row, 0], own[slot(0)], preferred_element_type=jnp.float32)
        total += jnp.dot(blocks_ref[row, 3], own[slot(3)], preferred_element_type=jnp.float32)
        total += jnp.dot(blocks_ref[row, 4], own[slot(4)], preferred_element_type=jnp.float32)
        total += jnp.dot(blocks_ref[row, near_side], near[slot(near_side)], preferred_element_type=jnp.float32)
        total += jnp.dot(blocks_ref[row, far_side], far[slot(far_side)], preferred_element_type=jnp.float32)
        if not first:
            total = 2.0 * total - before[k // GY][k % GY].astype(jnp.float32)
        if last:
            made[k] = total.astype(jnp.bfloat16)
            width = made.shape[2]
            copy = pltpu.make_async_copy(
                made.at[k], out_ref.at[row, :, pl.ds(column, width)], left.at[k]
            )
            copy.start()
            sent.append(copy)
        else:
            target = new_outer if k < GY else new_inner
            target[k % GY] = total.astype(jnp.bfloat16)
    for copy in sent:
        copy.wait()


def apply_step(odd, links, blocks, halos, current, before, out=None, column=0, out_shape=None):
    basis, width = current[0].shape[1:]
    last = out_shape is not None
    smem = pl.BlockSpec(memory_space=pltpu.SMEM)
    vmem = pl.BlockSpec(memory_space=pltpu.VMEM)
    anywhere = pl.BlockSpec(memory_space=pl.ANY)
    operands = [odd, links, blocks, halos[0], current[0], current[1], halos[1]]
    specs = [smem, smem] + [vmem] * 5
    if before is not None:
        operands += list(before)
        specs += [vmem] * 2
    aliases = {}
    scratch = []
    if last:
        if out is not None:
            aliases = {len(operands): 0}
            operands.append(out)
            specs.append(anywhere)
        shapes = jax.ShapeDtypeStruct(out_shape, jnp.bfloat16)
        out_specs = anywhere
        scratch += [
            pltpu.VMEM((2 * GY, basis, width), jnp.bfloat16),
            pltpu.SemaphoreType.DMA((2 * GY,)),
        ]
    else:
        shapes = [jax.ShapeDtypeStruct((GY, basis, width), jnp.bfloat16)] * 2
        out_specs = [vmem, vmem]
    flops = 2 * 2 * GY * blocks.shape[1] * basis * basis * width
    moved = 2 * blocks.size + 2 * 10 * GY * basis * width
    return pl.pallas_call(
        functools.partial(step_kernel, before is None, last, column),
        out_shape=shapes,
        in_specs=specs,
        out_specs=out_specs,
        scratch_shapes=scratch,
        input_output_aliases=aliases,
        compiler_params=pltpu.CompilerParams(vmem_limit_bytes=16 * MIB),
        cost_estimate=pl.CostEstimate(flops=flops, bytes_accessed=moved, transcendentals=0),
    )(*operands)


def rotate_kernel(count, *refs):
    pieces, matrix, outs = refs[:count], refs[count], refs[count + 1 :]
    for k in range(GY):
        row = 0
        total = None
        for piece in pieces:
            width = piece.shape[2]
            part = jnp.dot(piece[k], matrix[row : row + width, :], preferred_element_type=jnp.float32)
            total = part if total is None else total + part
            row += width
        column = 0
        for out in outs:
            width = out.shape[2]
            out[k] = total[:, column : column + width].astype(jnp.bfloat16)
            column += width


def rotate(pieces, matrix, widths):
    basis = pieces[0].shape[1]
    vmem = pl.BlockSpec(memory_space=pltpu.VMEM)
    flops = 2 * GY * basis * matrix.shape[0] * matrix.shape[1]
    moved = 2 * (matrix.size + GY * basis * (matrix.shape[0] + matrix.shape[1]))
    return pl.pallas_call(
        functools.partial(rotate_kernel, len(pieces)),
        out_shape=[jax.ShapeDtypeStruct((GY, basis, width), jnp.bfloat16) for width in widths],
        in_specs=[vmem] * (len(pieces) + 1),
        out_specs=[vmem] * len(widths),
        compiler_params=pltpu.CompilerParams(vmem_limit_bytes=16 * MIB),
        cost_estimate=pl.CostEstimate(flops=flops, bytes_accessed=moved, transcendentals=0),
    )(*pieces, matrix)


def exchange(array, axis, partner):
    return lax.ppermute(array, axis, [(i, partner(i)) for i in range(lax.axis_size(axis))])


def gathered_rotation(rotation, band_order):
    elems, bands = lax.axis_size("elem"), lax.axis_size("band")
    me = lax.axis_index("elem")
    bits = [1 << b for b in range(elems.bit_length() - 1)]
    bits = bits[1:] + bits[:1]
    owners = [0]
    rows = rotation
    for bit in bits:
        rows = jnp.concatenate([rows, exchange(rows, "elem", lambda i: i ^ bit)], axis=0)
        owners = owners + [owner ^ bit for owner in owners]
    share = rotation.shape[0]
    order = band_order.reshape(elems, share)[jnp.bitwise_xor(me, jnp.array(owners))].reshape(-1)
    total = order.shape[0]
    width = total // bands
    place = lax.iota(jnp.int32, total)
    band = jnp.bitwise_xor(place // width, lax.axis_index("band")) * width + place % width
    choice = (band[:, None] == order[None, :]).astype(jnp.bfloat16)
    return jnp.dot(choice, rows, preferred_element_type=jnp.float32).astype(jnp.bfloat16)


def body(start_bands, blocks, neighbours, band_order, rotation):
    elem_count, basis, width = start_bands.shape
    assert elem_count == 2 * GY
    elems, bands = lax.axis_size("elem"), lax.axis_size("band")
    odd = lax.axis_index("elem") % 2
    odd_flag = odd.astype(jnp.int32).reshape(1)
    chunk = min(CHUNK, width)
    starts = list(range(0, width, chunk))
    widths = [chunk] * len(starts)

    def cross(array):
        return exchange(array, "elem", lambda i: (i - 1) % elems if i % 2 == 0 else (i + 1) % elems)

    def intra(array):
        return exchange(array, "elem", lambda i: i ^ 1)

    def step(current, before, **output):
        halos = (cross(current[0]), intra(current[1]))
        return apply_step(odd_flag, neighbours, blocks, halos, current, before, **output)

    matrix = gathered_rotation(rotation, band_order)

    state = []
    for column in starts:
        part = lax.slice_in_dim(start_bands, column, column + chunk, axis=2)
        state.append(
            (
                lax.dynamic_slice_in_dim(part, odd * GY, GY, axis=0),
                lax.dynamic_slice_in_dim(part, (1 - odd) * GY, GY, axis=0),
            )
        )
    before = [None] * len(starts)
    for _ in range(3):
        for c in range(len(starts)):
            new = step(state[c], before[c])
            before[c], state[c] = state[c], tuple(new)

    rotated = []
    for side in range(2):
        own = [state[c][side] for c in range(len(starts))]
        pieces = list(own)
        for shift in range(1, bands):
            pieces += [exchange(piece, "band", lambda i: i ^ shift) for piece in own]
        rotated.append(rotate(pieces, matrix, widths))
    state = [(rotated[0][c], rotated[1][c]) for c in range(len(starts))]

    before = [None] * len(starts)
    for _ in range(2):
        for c in range(len(starts)):
            new = step(state[c], before[c])
            before[c], state[c] = state[c], tuple(new)
    out = None
    for c in range(len(starts)):
        out = step(state[c], before[c], out=out, column=starts[c], out_shape=start_bands.shape)
    return out


def solution(mesh):
    return jax.shard_map(
        body,
        mesh=mesh,
        in_specs=(
            P("elem", None, "band"),
            P("elem", None, None, None),
            P("elem", None),
            P(),
            P("elem", "band"),
        ),
        out_specs=P("elem", None, "band"),
        check_vma=False,
    )
```

```python
import functools

import jax
import jax.numpy as jnp
from jax import lax
from jax.experimental import pallas as pl
from jax.experimental.pallas import tpu as pltpu
from jax.sharding import PartitionSpec as P

GY = 3
CHUNK = 256
MIB = 1024 * 1024
LONG = 4 * 10**9
PARAMS = pltpu.CompilerParams(vmem_limit_bytes=16 * MIB)
SMEM = pl.BlockSpec(memory_space=pltpu.SMEM)
VMEM = pl.BlockSpec(memory_space=pltpu.VMEM)
ANYWHERE = pl.BlockSpec(memory_space=pl.ANY)
HBM = pl.BlockSpec(memory_space=pltpu.HBM)


def cost(flops):
    return pl.CostEstimate(flops=flops, bytes_accessed=1024, transcendentals=0)


def like(array):
    return jax.ShapeDtypeStruct(array.shape, array.dtype)


def bands_of(count, basis, width):
    return jax.ShapeDtypeStruct((count, basis, width), jnp.bfloat16)


def first_row(side, odd):
    return odd * GY if side == 0 else (1 - odd) * GY


def run_copies(pairs, sems):
    copies = [pltpu.make_async_copy(source, target, sems.at[n]) for n, (source, target) in enumerate(pairs)]
    for copy in copies:
        copy.start()
    return copies


def split_kernel(starts, width, held, waits, odd_ref, start_ref, *refs):
    refs = list(refs)
    pairs = []
    if held:
        blocks_ref, refs = refs[0], refs[1:]
    refs = refs[waits:]
    sems = refs.pop()
    if held:
        pairs.append((blocks_ref, refs.pop(0)))
    for n, target in enumerate(refs):
        rows = pl.ds(first_row(n % 2, odd_ref[0]), GY)
        pairs.append((start_ref.at[rows, :, pl.ds(starts[n // 2], width)], target))
    for copy in run_copies(pairs, sems):
        copy.wait()


def split(odd, start_bands, starts, width, blocks=None, later=()):
    basis = start_bands.shape[1]
    held = [] if blocks is None else [blocks]
    shapes = [pltpu.VMEM(b.shape, b.dtype) for b in held] + [bands_of(GY, basis, width)] * (2 * len(starts))
    result = pl.pallas_call(
        functools.partial(split_kernel, starts, width, len(held), len(later)),
        out_shape=shapes,
        in_specs=[SMEM, HBM] + [HBM] * len(held) + [ANYWHERE] * len(later),
        out_specs=[VMEM] * len(shapes),
        scratch_shapes=[pltpu.SemaphoreType.DMA((len(shapes),))],
        compiler_params=PARAMS,
        cost_estimate=cost(LONG),
    )(odd, start_bands, *held, *later)
    parts = result[len(held) :]
    return result[: len(held)], [[parts[2 * n], parts[2 * n + 1]] for n in range(len(starts))]


def step_kernel(sides, firsts, out_column, has_out, waits, joined, odd_ref, links_ref, blocks_ref, *refs):
    refs = list(refs)

    def take(count):
        taken = refs[:count]
        del refs[:count]
        return taken

    current = take(2)
    halos = take(len(sides))
    before = [None if first else take(1)[0] for first in firsts]
    join = take(2 * joined)
    take(waits + has_out)
    results = take(1 if out_column is not None else len(sides))
    join_out = take(joined)
    if out_column is not None:
        made, left = take(2)
    copies = []
    if joined:
        rows = join[0].shape[0]
        copies = run_copies([(join[0], join_out[0].at[:rows]), (join[1], join_out[0].at[rows:])], refs[0])
    odd = odd_ref[0]
    for i, side in enumerate(sides):
        far_side = 1 + odd if side == 0 else 2 - odd
        near_side = 3 - far_side
        for k in range(GY):
            row = first_row(side, odd) + k

            def term(s, column):
                slot = lax.rem(links_ref[row, s], GY)
                return jnp.dot(blocks_ref[row, s], column[slot], preferred_element_type=jnp.float32)

            total = term(0, current[side])
            total += term(3, current[side])
            total += term(4, current[side])
            total += term(near_side, current[1 - side])
            total += term(far_side, halos[i])
            if before[i] is not None:
                total = 2.0 * total - before[i][k].astype(jnp.float32)
            if out_column is None:
                results[i][k] = total.astype(jnp.bfloat16)
            else:
                n = i * GY + k
                made[n] = total.astype(jnp.bfloat16)
                place = results[0].at[row, :, pl.ds(out_column, made.shape[2])]
                copy = pltpu.make_async_copy(made.at[n], place, left.at[n])
                copy.start()
                copies.append(copy)
    for copy in copies:
        copy.wait()


def apply_step(shared, sides, current, halos, before, out=None, out_column=None, out_shape=None, later=(), join=()):
    basis, width = current[0].shape[1:]
    operands = list(shared) + list(current) + list(halos) + [b for b in before if b is not None] + list(join)
    specs = [SMEM, SMEM] + [VMEM] * (len(operands) - 2) + [ANYWHERE] * len(later)
    operands += list(later)
    aliases, scratch = {}, []
    if out_column is None:
        shapes = [bands_of(GY, basis, width)] * len(sides)
        out_specs = [VMEM] * len(sides)
    else:
        if out is not None:
            aliases = {len(operands): 0}
            operands.append(out)
            specs.append(ANYWHERE)
        shapes, out_specs = [jax.ShapeDtypeStruct(out_shape, jnp.bfloat16)], [ANYWHERE]
        parts = len(sides) * GY
        scratch = [pltpu.VMEM((parts, basis, width), jnp.bfloat16), pltpu.SemaphoreType.DMA((parts,))]
    if join:
        rows = join[0].shape[0] + join[1].shape[0]
        shapes.append(jax.ShapeDtypeStruct((rows,) + join[0].shape[1:], join[0].dtype))
        out_specs.append(VMEM)
        scratch.append(pltpu.SemaphoreType.DMA((2,)))
    firsts = [b is None for b in before]
    return pl.pallas_call(
        functools.partial(step_kernel, sides, firsts, out_column, out is not None, len(later), int(bool(join))),
        out_shape=shapes,
        in_specs=specs,
        out_specs=out_specs,
        scratch_shapes=scratch,
        input_output_aliases=aliases,
        compiler_params=PARAMS,
        cost_estimate=cost(LONG),
    )(*operands)


def rotate_kernel(count, column, extra, passed, *refs):
    pieces, matrix = refs[:count], refs[count]
    outs = refs[count + 1 + extra : len(refs) - passed]
    for k in range(GY):
        rows = jnp.concatenate([piece[k] for piece in pieces], axis=1)
        start = column
        for out in outs:
            width = out.shape[2]
            out[k] = jnp.dot(
                rows, matrix[:, start : start + width], preferred_element_type=jnp.float32
            ).astype(jnp.bfloat16)
            start += width


def rotate(pieces, matrix, column, widths, passed=(), later=()):
    basis = pieces[0].shape[1]
    count = len(pieces) + 1
    result = pl.pallas_call(
        functools.partial(rotate_kernel, len(pieces), column, len(passed) + len(later), len(passed)),
        out_shape=[bands_of(GY, basis, width) for width in widths] + [like(p) for p in passed],
        in_specs=[VMEM] * count + [ANYWHERE] * (len(passed) + len(later)),
        out_specs=[VMEM] * len(widths) + [ANYWHERE] * len(passed),
        input_output_aliases={count + i: len(widths) + i for i in range(len(passed))},
        compiler_params=PARAMS,
        cost_estimate=cost(LONG // 2),
    )(*pieces, matrix, *passed, *later)
    return list(result[: len(widths)]), list(result[len(widths) :])


def ordered_kernel(bands, own_ref, order_ref, *refs):
    rows, out_ref = refs[:-1], refs[-1]
    total = out_ref.shape[0]
    width = total // bands
    for shift in range(bands):
        for start in range(0, width, 256):
            size = min(256, width - start)
            first = jnp.bitwise_xor(own_ref[0], shift) * width + start
            band = lax.broadcasted_iota(jnp.int32, (size, total), 0) + first
            choice = (band == order_ref[...]).astype(jnp.float32).astype(jnp.bfloat16)
            result, column = None, 0
            for part in rows:
                held = choice[:, column : column + part.shape[0]]
                found = jnp.dot(held, part[...], preferred_element_type=jnp.float32)
                result = found if result is None else result + found
                column += part.shape[0]
            place = shift * width + start
            out_ref[place : place + size, :] = result.astype(jnp.bfloat16)


def ordered_rows(own, order, rows, bands):
    total = order.shape[1]
    return pl.pallas_call(
        functools.partial(ordered_kernel, bands),
        out_shape=jax.ShapeDtypeStruct((total, rows[0].shape[1]), rows[0].dtype),
        in_specs=[SMEM] + [VMEM] * (1 + len(rows)),
        out_specs=VMEM,
        compiler_params=PARAMS,
        cost_estimate=cost(LONG // 2),
    )(own, order, *rows)


def exchange(array, axis, partner):
    return lax.ppermute(array, axis, [(i, partner(i)) for i in range(lax.axis_size(axis))])


class Gather:
    def __init__(self, rows):
        elems = lax.axis_size("elem")
        bits = [1 << b for b in range(elems.bit_length() - 1)]
        self.bits = bits[1:2] + bits[:1:-1] + bits[:1]
        self.owners = [0]
        self.held = rows
        self.received = self.send()

    def send(self):
        bit = self.bits.pop(0)
        self.owners = self.owners + [owner ^ bit for owner in self.owners]
        return exchange(self.held, "elem", lambda i: i ^ bit)

    def parts(self):
        return [self.held, self.received]

    def step(self, *args, **kwargs):
        if not self.bits:
            return apply_step(*args, **kwargs)
        result = apply_step(*args, join=self.parts(), **kwargs)
        self.held = result[-1]
        self.received = self.send()
        return result[:-1]

    def finish(self):
        while self.bits:
            self.held = jnp.concatenate(self.parts(), axis=0)
            self.received = self.send()
        return self.parts(), jnp.array(self.owners)


def body(start_bands, blocks, neighbours, band_order, rotation):
    elem_count, basis, width = start_bands.shape
    assert elem_count == 2 * GY
    elems, bands = lax.axis_size("elem"), lax.axis_size("band")
    me = lax.axis_index("elem")
    odd = (me % 2).astype(jnp.int32).reshape(1)
    chunk = min(CHUNK, width)
    starts = list(range(0, width, chunk))
    chunks = range(len(starts))
    nothing = [None, None]

    def cross(array):
        return exchange(array, "elem", lambda i: (i - 1) % elems if i % 2 == 0 else (i + 1) % elems)

    def intra(array):
        return exchange(array, "elem", lambda i: i ^ 1)

    def halos(columns):
        return [cross(columns[0]), intra(columns[1])]

    def over_band(piece):
        return [exchange(piece, "band", lambda i: i ^ shift) for shift in range(1, bands)]

    _, state = split(odd, start_bands, starts[:1], chunk)
    beside = [halos(state[0])]
    (held,), rest = split(odd, start_bands, starts[1:], chunk, blocks, later=beside[0][1:])
    state += rest
    beside += [halos(columns) for columns in rest]
    shared = (odd, neighbours, held)
    gather = Gather(rotation)

    before = [nothing for _ in chunks]
    for _ in range(2):
        for c in chunks:
            step = gather.step if c == 0 else apply_step
            new = step(shared, (0, 1), state[c], beside[c], before[c], later=state[c - 1][:1] if c or before[0][0] is not None else ())
            before[c], state[c] = state[c], new
            beside[c] = halos(new)

    inner, inner_others, outer, outer_others = [], [], [], []
    waits = []
    for c in chunks:
        step = gather.step if c == 0 else apply_step
        inner += apply_step(shared, (1,), state[c], beside[c][1:], before[c][1:], later=outer[-1:])
        outer += step(shared, (0,), state[c], beside[c][:1], before[c][:1], later=waits + inner[-1:])
        outer_others.append(over_band(outer[-1]))
        if c != chunks[-1]:
            inner_others.append(over_band(inner[-1]))
            waits = inner_others[-1]
    rows, owners = gather.finish()
    order = band_order.reshape(elems, -1)[jnp.bitwise_xor(me, owners)].reshape(1, -1)
    matrix = ordered_rows(lax.axis_index("band").astype(jnp.int32).reshape(1), order, rows, bands)

    def by_band(own, others):
        return list(own) + [other[shift] for shift in range(bands - 1) for other in others]

    pieces = by_band(outer, outer_others)
    rotated, last = rotate(pieces, matrix, 0, [chunk], passed=inner[-1:])
    far = [cross(rotated[0])]
    inner[-1] = last[0]
    inner_others.append(over_band(inner[-1]))
    for c in chunks[1:]:
        rotated += rotate(pieces, matrix, starts[c], [chunk], later=inner_others[-1])[0]
        far.append(cross(rotated[c]))
    rotated_inner, _ = rotate(by_band(inner, inner_others), matrix, 0, [chunk for _ in chunks])
    state = [[rotated[c], rotated_inner[c]] for c in chunks]
    beside = [[far[c], intra(rotated_inner[c])] for c in chunks]

    before = [nothing for _ in chunks]
    for _ in range(2):
        for c in chunks:
            new = apply_step(shared, (0, 1), state[c], beside[c], before[c])
            before[c], state[c] = state[c], new
            beside[c] = halos(new)
    out = None
    for c in chunks:
        (out,) = apply_step(
            shared, (0, 1), state[c], beside[c], before[c],
            out=out, out_column=starts[c], out_shape=start_bands.shape,
        )
    return out


def solution(mesh):
    return jax.shard_map(
        body,
        mesh=mesh,
        in_specs=(
            P("elem", None, "band"),
            P("elem", None, None, None),
            P("elem", None),
            P(),
            P("elem", "band"),
        ),
        out_specs=P("elem", None, "band"),
        check_vma=False,
    )
```

```python
import functools

import jax
import jax.numpy as jnp
from jax import lax
from jax.experimental import pallas as pl
from jax.experimental.pallas import tpu as pltpu
from jax.sharding import PartitionSpec as P

GY = 3
CHUNK = 256
MIB = 1024 * 1024
LONG = 4 * 10**9
PARAMS = pltpu.CompilerParams(vmem_limit_bytes=16 * MIB)
SMEM = pl.BlockSpec(memory_space=pltpu.SMEM)
VMEM = pl.BlockSpec(memory_space=pltpu.VMEM)
ANYWHERE = pl.BlockSpec(memory_space=pl.ANY)
HBM = pl.BlockSpec(memory_space=pltpu.HBM)


def cost(flops):
    return pl.CostEstimate(flops=flops, bytes_accessed=1024, transcendentals=0)


def like(array):
    return jax.ShapeDtypeStruct(array.shape, array.dtype)


def bands_of(count, basis, width):
    return jax.ShapeDtypeStruct((count, basis, width), jnp.bfloat16)


def first_row(side, odd):
    return odd * GY if side == 0 else (1 - odd) * GY


def run_copies(pairs, sems):
    copies = [pltpu.make_async_copy(source, target, sems.at[n]) for n, (source, target) in enumerate(pairs)]
    for copy in copies:
        copy.start()
    return copies


def split_kernel(starts, width, held, waits, odd_ref, start_ref, *refs):
    refs = list(refs)
    pairs = []
    if held:
        blocks_ref, refs = refs[0], refs[1:]
    refs = refs[waits:]
    sems = refs.pop()
    if held:
        pairs.append((blocks_ref, refs.pop(0)))
    for n, target in enumerate(refs):
        rows = pl.ds(first_row(n % 2, odd_ref[0]), GY)
        pairs.append((start_ref.at[rows, :, pl.ds(starts[n // 2], width)], target))
    for copy in run_copies(pairs, sems):
        copy.wait()


def split(odd, start_bands, starts, width, blocks=None, later=()):
    basis = start_bands.shape[1]
    held = [] if blocks is None else [blocks]
    shapes = [pltpu.VMEM(b.shape, b.dtype) for b in held] + [bands_of(GY, basis, width)] * (2 * len(starts))
    result = pl.pallas_call(
        functools.partial(split_kernel, starts, width, len(held), len(later)),
        out_shape=shapes,
        in_specs=[SMEM, HBM] + [HBM] * len(held) + [ANYWHERE] * len(later),
        out_specs=[VMEM] * len(shapes),
        scratch_shapes=[pltpu.SemaphoreType.DMA((len(shapes),))],
        compiler_params=PARAMS,
        cost_estimate=cost(LONG),
    )(odd, start_bands, *held, *later)
    parts = result[len(held) :]
    return result[: len(held)], [[parts[2 * n], parts[2 * n + 1]] for n in range(len(starts))]


def step_kernel(sides, firsts, out_column, has_out, waits, joined, odd_ref, links_ref, blocks_ref, *refs):
    refs = list(refs)

    def take(count):
        taken = refs[:count]
        del refs[:count]
        return taken

    current = take(2)
    halos = take(len(sides))
    before = [None if first else take(1)[0] for first in firsts]
    join = take(2 * joined)
    take(waits + has_out)
    results = take(1 if out_column is not None else len(sides))
    join_out = take(joined)
    if out_column is not None:
        made, left = take(2)
    copies = []
    if joined:
        rows = join[0].shape[0]
        copies = run_copies([(join[0], join_out[0].at[:rows]), (join[1], join_out[0].at[rows:])], refs[0])
    odd = odd_ref[0]
    for i, side in enumerate(sides):
        far_side = 1 + odd if side == 0 else 2 - odd
        near_side = 3 - far_side
        for k in range(GY):
            row = first_row(side, odd) + k

            def term(s, column):
                slot = lax.rem(links_ref[row, s], GY)
                return jnp.dot(blocks_ref[row, s], column[slot], preferred_element_type=jnp.float32)

            total = term(0, current[side])
            total += term(3, current[side])
            total += term(4, current[side])
            total += term(near_side, current[1 - side])
            total += term(far_side, halos[i])
            if before[i] is not None:
                total = 2.0 * total - before[i][k].astype(jnp.float32)
            if out_column is None:
                results[i][k] = total.astype(jnp.bfloat16)
            else:
                n = i * GY + k
                made[n] = total.astype(jnp.bfloat16)
                place = results[0].at[row, :, pl.ds(out_column, made.shape[2])]
                copy = pltpu.make_async_copy(made.at[n], place, left.at[n])
                copy.start()
                copies.append(copy)
    for copy in copies:
        copy.wait()


def apply_step(shared, sides, current, halos, before, out=None, out_column=None, out_shape=None, later=(), join=()):
    basis, width = current[0].shape[1:]
    operands = list(shared) + list(current) + list(halos) + [b for b in before if b is not None] + list(join)
    specs = [SMEM, SMEM] + [VMEM] * (len(operands) - 2) + [ANYWHERE] * len(later)
    operands += list(later)
    aliases, scratch = {}, []
    if out_column is None:
        shapes = [bands_of(GY, basis, width)] * len(sides)
        out_specs = [VMEM] * len(sides)
    else:
        if out is not None:
            aliases = {len(operands): 0}
            operands.append(out)
            specs.append(ANYWHERE)
        shapes, out_specs = [jax.ShapeDtypeStruct(out_shape, jnp.bfloat16)], [ANYWHERE]
        parts = len(sides) * GY
        scratch = [pltpu.VMEM((parts, basis, width), jnp.bfloat16), pltpu.SemaphoreType.DMA((parts,))]
    if join:
        rows = join[0].shape[0] + join[1].shape[0]
        shapes.append(jax.ShapeDtypeStruct((rows,) + join[0].shape[1:], join[0].dtype))
        out_specs.append(VMEM)
        scratch.append(pltpu.SemaphoreType.DMA((2,)))
    firsts = [b is None for b in before]
    return pl.pallas_call(
        functools.partial(step_kernel, sides, firsts, out_column, out is not None, len(later), int(bool(join))),
        out_shape=shapes,
        in_specs=specs,
        out_specs=out_specs,
        scratch_shapes=scratch,
        input_output_aliases=aliases,
        compiler_params=PARAMS,
        cost_estimate=cost(LONG),
    )(*operands)


def rotate_kernel(count, column, extra, passed, *refs):
    pieces, matrix = refs[:count], refs[count]
    outs = refs[count + 1 + extra : len(refs) - passed]
    for k in range(GY):
        rows = jnp.concatenate([piece[k] for piece in pieces], axis=1)
        start = column
        for out in outs:
            width = out.shape[2]
            out[k] = jnp.dot(
                rows, matrix[:, start : start + width], preferred_element_type=jnp.float32
            ).astype(jnp.bfloat16)
            start += width


def rotate(pieces, matrix, column, widths, passed=(), later=()):
    basis = pieces[0].shape[1]
    count = len(pieces) + 1
    result = pl.pallas_call(
        functools.partial(rotate_kernel, len(pieces), column, len(passed) + len(later), len(passed)),
        out_shape=[bands_of(GY, basis, width) for width in widths] + [like(p) for p in passed],
        in_specs=[VMEM] * count + [ANYWHERE] * (len(passed) + len(later)),
        out_specs=[VMEM] * len(widths) + [ANYWHERE] * len(passed),
        input_output_aliases={count + i: len(widths) + i for i in range(len(passed))},
        compiler_params=PARAMS,
        cost_estimate=cost(LONG // 2),
    )(*pieces, matrix, *passed, *later)
    return list(result[: len(widths)]), list(result[len(widths) :])


def ordered_kernel(bands, count, own_ref, order_ref, *refs):
    rows, out_ref = refs[:count], refs[-1]
    total = out_ref.shape[0]
    width = total // bands
    for shift in range(bands):
        for start in range(0, width, 256):
            size = min(256, width - start)
            first = jnp.bitwise_xor(own_ref[0], shift) * width + start
            band = lax.broadcasted_iota(jnp.int32, (size, total), 0) + first
            choice = (band == order_ref[...]).astype(jnp.float32).astype(jnp.bfloat16)
            result, column = None, 0
            for part in rows:
                held = choice[:, column : column + part.shape[0]]
                found = jnp.dot(held, part[...], preferred_element_type=jnp.float32)
                result = found if result is None else result + found
                column += part.shape[0]
            place = shift * width + start
            out_ref[place : place + size, :] = result.astype(jnp.bfloat16)


def ordered_rows(own, order, rows, bands, later):
    total = order.shape[1]
    return pl.pallas_call(
        functools.partial(ordered_kernel, bands, len(rows)),
        out_shape=jax.ShapeDtypeStruct((total, rows[0].shape[1]), rows[0].dtype),
        in_specs=[SMEM] + [VMEM] * (1 + len(rows)) + [ANYWHERE] * len(later),
        out_specs=VMEM,
        compiler_params=PARAMS,
        cost_estimate=cost(LONG),
    )(own, order, *rows, *later)


def exchange(array, axis, partner):
    return lax.ppermute(array, axis, [(i, partner(i)) for i in range(lax.axis_size(axis))])


class Gather:
    def __init__(self, rows):
        elems = lax.axis_size("elem")
        bits = [1 << b for b in range(elems.bit_length() - 1)]
        self.bits = bits[1:2] + bits[:1:-1] + bits[:1]
        self.owners = [0]
        self.held = rows
        self.received = self.send()

    def send(self):
        bit = self.bits.pop(0)
        self.owners = self.owners + [owner ^ bit for owner in self.owners]
        return exchange(self.held, "elem", lambda i: i ^ bit)

    def parts(self):
        return [self.held, self.received]

    def step(self, *args, **kwargs):
        if len(self.bits) < 2:
            return apply_step(*args, **kwargs)
        result = apply_step(*args, join=self.parts(), **kwargs)
        self.held = result[-1]
        self.received = self.send()
        return result[:-1]

    def finish(self):
        while len(self.bits) > 1:
            self.held = jnp.concatenate(self.parts(), axis=0)
            self.received = self.send()
        parts = self.parts()
        for bit in self.bits:
            parts = parts + [exchange(part, "elem", lambda i: i ^ bit) for part in parts]
            self.owners = self.owners + [owner ^ bit for owner in self.owners]
        return parts, jnp.array(self.owners)


def body(start_bands, blocks, neighbours, band_order, rotation):
    elem_count, basis, width = start_bands.shape
    assert elem_count == 2 * GY
    elems, bands = lax.axis_size("elem"), lax.axis_size("band")
    me = lax.axis_index("elem")
    odd = (me % 2).astype(jnp.int32).reshape(1)
    chunk = min(CHUNK, width)
    starts = list(range(0, width, chunk))
    chunks = range(len(starts))
    nothing = [None, None]

    def cross(array):
        return exchange(array, "elem", lambda i: (i - 1) % elems if i % 2 == 0 else (i + 1) % elems)

    def intra(array):
        return exchange(array, "elem", lambda i: i ^ 1)

    def halos(columns):
        return [cross(columns[0]), intra(columns[1])]

    def over_band(piece):
        return [exchange(piece, "band", lambda i: i ^ shift) for shift in range(1, bands)]

    place = (me % 2) * GY
    state = [
        [
            lax.dynamic_slice(start_bands, (first, 0, starts[0]), (GY, basis, chunk))
            for first in (place, GY - place)
        ]
    ]
    beside = [halos(state[0])]
    (held,), rest = split(odd, start_bands, starts[1:], chunk, blocks, later=beside[0][1:])
    state += rest
    beside += [halos(columns) for columns in rest]
    shared = (odd, neighbours, held)
    gather = Gather(rotation)

    before = [nothing for _ in chunks]
    for n in range(2):
        for c in chunks:
            step = gather.step if c == (chunks[0], chunks[-1])[n] else apply_step
            new = step(shared, (0, 1), state[c], beside[c], before[c], later=state[c - 1][:1] if c or before[0][0] is not None else ())
            before[c], state[c] = state[c], new
            beside[c] = halos(new)

    inner, inner_others, outer, outer_others = [], [], [], []
    waits = []
    for c in chunks:
        step = gather.step if c == chunks[-1] else apply_step
        inner += apply_step(shared, (1,), state[c], beside[c][1:], before[c][1:], later=outer[-1:])
        outer += step(shared, (0,), state[c], beside[c][:1], before[c][:1], later=waits + inner[-1:])
        outer_others.append(over_band(outer[-1]))
        if c != chunks[-1]:
            inner_others.append(over_band(inner[-1]))
            waits = inner_others[-1]
        if c == 0:
            rows, owners = gather.finish()
    order = band_order.reshape(elems, -1)[jnp.bitwise_xor(me, owners)].reshape(1, -1)
    matrix = ordered_rows(lax.axis_index("band").astype(jnp.int32).reshape(1), order, rows, bands, later=outer_others[0])

    def by_band(own, others):
        return list(own) + [other[shift] for shift in range(bands - 1) for other in others]

    pieces = by_band(outer, outer_others)
    rotated, last = rotate(pieces, matrix, 0, [chunk], passed=inner[-1:])
    far = [cross(rotated[0])]
    inner[-1] = last[0]
    inner_others.append(over_band(inner[-1]))
    for c in chunks[1:]:
        rotated += rotate(pieces, matrix, starts[c], [chunk], later=inner_others[-1])[0]
        far.append(cross(rotated[c]))
    rotated_inner, _ = rotate(by_band(inner, inner_others), matrix, 0, [chunk for _ in chunks])
    state = [[rotated[c], rotated_inner[c]] for c in chunks]
    beside = [[far[c], intra(rotated_inner[c])] for c in chunks]

    before = [nothing for _ in chunks]
    for _ in range(2):
        for c in chunks:
            new = apply_step(shared, (0, 1), state[c], beside[c], before[c])
            before[c], state[c] = state[c], new
            beside[c] = halos(new)
    out = None
    for c in chunks:
        (out,) = apply_step(
            shared, (0, 1), state[c], beside[c], before[c],
            out=out, out_column=starts[c], out_shape=start_bands.shape,
        )
    return out


def solution(mesh):
    return jax.shard_map(
        body,
        mesh=mesh,
        in_specs=(
            P("elem", None, "band"),
            P("elem", None, None, None),
            P("elem", None),
            P(),
            P("elem", "band"),
        ),
        out_specs=P("elem", None, "band"),
        check_vma=False,
    )
```

```python
import functools

import jax
import jax.numpy as jnp
from jax import lax
from jax.experimental import pallas as pl
from jax.experimental.pallas import tpu as pltpu
from jax.sharding import PartitionSpec as P

GY = 3
CHUNK = 256
MIB = 1024 * 1024
LONG = 4 * 10**9
PARAMS = pltpu.CompilerParams(vmem_limit_bytes=16 * MIB)
SMEM = pl.BlockSpec(memory_space=pltpu.SMEM)
VMEM = pl.BlockSpec(memory_space=pltpu.VMEM)
ANYWHERE = pl.BlockSpec(memory_space=pl.ANY)
HBM = pl.BlockSpec(memory_space=pltpu.HBM)


def cost(flops):
    return pl.CostEstimate(flops=flops, bytes_accessed=1024, transcendentals=0)


def like(array):
    return jax.ShapeDtypeStruct(array.shape, array.dtype)


def bands_of(count, basis, width):
    return jax.ShapeDtypeStruct((count, basis, width), jnp.bfloat16)


def first_row(side, odd):
    return odd * GY if side == 0 else (1 - odd) * GY


def run_copies(pairs, sems):
    copies = [pltpu.make_async_copy(source, target, sems.at[n]) for n, (source, target) in enumerate(pairs)]
    for copy in copies:
        copy.start()
    return copies


def split_kernel(starts, width, held, waits, odd_ref, start_ref, *refs):
    refs = list(refs)
    pairs = []
    if held:
        blocks_ref, refs = refs[0], refs[1:]
    refs = refs[waits:]
    sems = refs.pop()
    if held:
        pairs.append((blocks_ref, refs.pop(0)))
    for n, target in enumerate(refs):
        rows = pl.ds(first_row(n % 2, odd_ref[0]), GY)
        pairs.append((start_ref.at[rows, :, pl.ds(starts[n // 2], width)], target))
    for copy in run_copies(pairs, sems):
        copy.wait()


def split(odd, start_bands, starts, width, blocks=None, later=()):
    basis = start_bands.shape[1]
    held = [] if blocks is None else [blocks]
    shapes = [pltpu.VMEM(b.shape, b.dtype) for b in held] + [bands_of(GY, basis, width)] * (2 * len(starts))
    result = pl.pallas_call(
        functools.partial(split_kernel, starts, width, len(held), len(later)),
        out_shape=shapes,
        in_specs=[SMEM, HBM] + [HBM] * len(held) + [ANYWHERE] * len(later),
        out_specs=[VMEM] * len(shapes),
        scratch_shapes=[pltpu.SemaphoreType.DMA((len(shapes),))],
        compiler_params=PARAMS,
        cost_estimate=cost(LONG),
    )(odd, start_bands, *held, *later)
    parts = result[len(held) :]
    return result[: len(held)], [[parts[2 * n], parts[2 * n + 1]] for n in range(len(starts))]


def step_kernel(sides, firsts, out_column, has_out, waits, joined, odd_ref, links_ref, blocks_ref, *refs):
    refs = list(refs)

    def take(count):
        taken = refs[:count]
        del refs[:count]
        return taken

    current = take(2)
    halos = take(len(sides))
    before = [None if first else take(1)[0] for first in firsts]
    join = take(2 * joined)
    take(waits + has_out)
    results = take(1 if out_column is not None else len(sides))
    join_out = take(joined)
    if out_column is not None:
        made, left = take(2)
    copies = []
    if joined:
        rows = join[0].shape[0]
        copies = run_copies([(join[0], join_out[0].at[:rows]), (join[1], join_out[0].at[rows:])], refs[0])
    odd = odd_ref[0]
    for i, side in enumerate(sides):
        far_side = 1 + odd if side == 0 else 2 - odd
        near_side = 3 - far_side
        for k in range(GY):
            row = first_row(side, odd) + k

            def term(s, column):
                slot = lax.rem(links_ref[row, s], GY)
                return jnp.dot(blocks_ref[row, s], column[slot], preferred_element_type=jnp.float32)

            total = term(0, current[side])
            total += term(3, current[side])
            total += term(4, current[side])
            total += term(near_side, current[1 - side])
            total += term(far_side, halos[i])
            if before[i] is not None:
                total = 2.0 * total - before[i][k].astype(jnp.float32)
            if out_column is None:
                results[i][k] = total.astype(jnp.bfloat16)
            else:
                n = i * GY + k
                made[n] = total.astype(jnp.bfloat16)
                place = results[0].at[row, :, pl.ds(out_column, made.shape[2])]
                copy = pltpu.make_async_copy(made.at[n], place, left.at[n])
                copy.start()
                copies.append(copy)
    for copy in copies:
        copy.wait()


def apply_step(shared, sides, current, halos, before, out=None, out_column=None, out_shape=None, later=(), join=()):
    basis, width = current[0].shape[1:]
    operands = list(shared) + list(current) + list(halos) + [b for b in before if b is not None] + list(join)
    specs = [SMEM, SMEM] + [VMEM] * (len(operands) - 2) + [ANYWHERE] * len(later)
    operands += list(later)
    aliases, scratch = {}, []
    if out_column is None:
        shapes = [bands_of(GY, basis, width)] * len(sides)
        out_specs = [VMEM] * len(sides)
    else:
        if out is not None:
            aliases = {len(operands): 0}
            operands.append(out)
            specs.append(ANYWHERE)
        shapes, out_specs = [jax.ShapeDtypeStruct(out_shape, jnp.bfloat16)], [ANYWHERE]
        parts = len(sides) * GY
        scratch = [pltpu.VMEM((parts, basis, width), jnp.bfloat16), pltpu.SemaphoreType.DMA((parts,))]
    if join:
        rows = join[0].shape[0] + join[1].shape[0]
        shapes.append(jax.ShapeDtypeStruct((rows,) + join[0].shape[1:], join[0].dtype))
        out_specs.append(VMEM)
        scratch.append(pltpu.SemaphoreType.DMA((2,)))
    firsts = [b is None for b in before]
    return pl.pallas_call(
        functools.partial(step_kernel, sides, firsts, out_column, out is not None, len(later), int(bool(join))),
        out_shape=shapes,
        in_specs=specs,
        out_specs=out_specs,
        scratch_shapes=scratch,
        input_output_aliases=aliases,
        compiler_params=PARAMS,
        cost_estimate=cost(LONG),
    )(*operands)


def rotate_kernel(count, column, extra, passed, *refs):
    pieces, matrix = refs[:count], refs[count]
    outs = refs[count + 1 + extra : len(refs) - passed]
    for k in range(GY):
        rows = jnp.concatenate([piece[k] for piece in pieces], axis=1)
        start = column
        for out in outs:
            width = out.shape[2]
            out[k] = jnp.dot(
                rows, matrix[:, start : start + width], preferred_element_type=jnp.float32
            ).astype(jnp.bfloat16)
            start += width


def rotate(pieces, matrix, column, widths, passed=(), later=()):
    basis = pieces[0].shape[1]
    count = len(pieces) + 1
    result = pl.pallas_call(
        functools.partial(rotate_kernel, len(pieces), column, len(passed) + len(later), len(passed)),
        out_shape=[bands_of(GY, basis, width) for width in widths] + [like(p) for p in passed],
        in_specs=[VMEM] * count + [ANYWHERE] * (len(passed) + len(later)),
        out_specs=[VMEM] * len(widths) + [ANYWHERE] * len(passed),
        input_output_aliases={count + i: len(widths) + i for i in range(len(passed))},
        compiler_params=PARAMS,
        cost_estimate=cost(LONG // 2),
    )(*pieces, matrix, *passed, *later)
    return list(result[: len(widths)]), list(result[len(widths) :])


def wait_kernel(*refs):
    del refs


def after(arrays, later):
    count = len(arrays)
    return pl.pallas_call(
        wait_kernel,
        out_shape=[like(array) for array in arrays],
        in_specs=[ANYWHERE] * (count + len(later)),
        out_specs=[ANYWHERE] * count,
        input_output_aliases={i: i for i in range(count)},
        compiler_params=PARAMS,
        cost_estimate=cost(LONG),
    )(*arrays, *later)


def ordered_kernel(bands, count, own_ref, order_ref, *refs):
    rows, out_ref = refs[:count], refs[-1]
    total = out_ref.shape[0]
    width = total // bands
    for shift in range(bands):
        for start in range(0, width, 256):
            size = min(256, width - start)
            first = jnp.bitwise_xor(own_ref[0], shift) * width + start
            band = lax.broadcasted_iota(jnp.int32, (size, total), 0) + first
            choice = (band == order_ref[...]).astype(jnp.float32).astype(jnp.bfloat16)
            result, column = None, 0
            for part in rows:
                held = choice[:, column : column + part.shape[0]]
                found = jnp.dot(held, part[...], preferred_element_type=jnp.float32)
                result = found if result is None else result + found
                column += part.shape[0]
            place = shift * width + start
            out_ref[place : place + size, :] = result.astype(jnp.bfloat16)


def ordered_rows(own, order, rows, bands, later):
    total = order.shape[1]
    return pl.pallas_call(
        functools.partial(ordered_kernel, bands, len(rows)),
        out_shape=jax.ShapeDtypeStruct((total, rows[0].shape[1]), rows[0].dtype),
        in_specs=[SMEM] + [VMEM] * (1 + len(rows)) + [ANYWHERE] * len(later),
        out_specs=VMEM,
        compiler_params=PARAMS,
        cost_estimate=cost(LONG),
    )(own, order, *rows, *later)


def exchange(array, axis, partner):
    return lax.ppermute(array, axis, [(i, partner(i)) for i in range(lax.axis_size(axis))])


class Gather:
    def __init__(self, rows):
        elems = lax.axis_size("elem")
        bits = [1 << b for b in range(elems.bit_length() - 1)]
        self.bits = bits[1:2] + bits[:1:-1] + bits[:1]
        self.owners = [0]
        self.held = rows
        self.received = self.send()

    def send(self):
        bit = self.bits.pop(0)
        self.owners = self.owners + [owner ^ bit for owner in self.owners]
        return exchange(self.held, "elem", lambda i: i ^ bit)

    def parts(self):
        return [self.held, self.received]

    def step(self, *args, **kwargs):
        if len(self.bits) < 2:
            return apply_step(*args, **kwargs)
        result = apply_step(*args, join=self.parts(), **kwargs)
        self.held = result[-1]
        self.received = self.send()
        return result[:-1]

    def finish(self):
        while len(self.bits) > 1:
            self.held = jnp.concatenate(self.parts(), axis=0)
            self.received = self.send()
        parts = self.parts()
        for bit in self.bits:
            parts = parts + [exchange(part, "elem", lambda i: i ^ bit) for part in parts]
            self.owners = self.owners + [owner ^ bit for owner in self.owners]
        return parts, jnp.array(self.owners)


def body(start_bands, blocks, neighbours, band_order, rotation):
    elem_count, basis, width = start_bands.shape
    assert elem_count == 2 * GY
    elems, bands = lax.axis_size("elem"), lax.axis_size("band")
    me = lax.axis_index("elem")
    odd = (me % 2).astype(jnp.int32).reshape(1)
    chunk = min(CHUNK, width)
    starts = list(range(0, width, chunk))
    chunks = range(len(starts))
    nothing = [None, None]

    def cross(array):
        return exchange(array, "elem", lambda i: (i - 1) % elems if i % 2 == 0 else (i + 1) % elems)

    def intra(array):
        return exchange(array, "elem", lambda i: i ^ 1)

    def halos(columns):
        return [cross(columns[0]), intra(columns[1])]

    def over_band(piece):
        return [exchange(piece, "band", lambda i: i ^ shift) for shift in range(1, bands)]

    place = (me % 2) * GY
    state = [
        [
            lax.dynamic_slice(start_bands, (first, 0, starts[0]), (GY, basis, chunk))
            for first in (place, GY - place)
        ]
    ]
    beside = [halos(state[0])]
    (held,), rest = split(odd, start_bands, starts[1:], chunk, blocks, later=beside[0][1:])
    state += rest
    beside += [halos(columns) for columns in rest]
    shared = (odd, neighbours, held)
    gather = Gather(rotation)

    before = [nothing for _ in chunks]
    for n in range(2):
        for c in chunks:
            step = gather.step if (n, c) in ((0, 0), (1, chunks[-1])) else apply_step
            new = step(shared, (0, 1), state[c], beside[c], before[c], later=state[c - 1][:1] if c or before[0][0] is not None else ())
            before[c], state[c] = state[c], new
            beside[c] = halos(new)

    inner, outer, outer_others = [], [], []
    for c in chunks:
        made = apply_step(shared, (0, 1), state[c], beside[c], before[c], later=state[c - 1][:1] if c == 0 else outer[-1:])
        outer.append(made[0])
        inner.append(made[1])
        outer_others.append(over_band(made[0]))
    rows, owners = gather.finish()
    inner = after(inner, outer_others[0])
    order = band_order.reshape(elems, -1)[jnp.bitwise_xor(me, owners)].reshape(1, -1)
    matrix = ordered_rows(lax.axis_index("band").astype(jnp.int32).reshape(1), order, rows, bands, later=outer_others[-1] + list(inner[:1]))

    def by_band(own, others):
        return list(own) + [other[shift] for shift in range(bands - 1) for other in others]

    pieces = by_band(outer, outer_others)
    rotated, inner = rotate(pieces, matrix, 0, [chunk], passed=inner)
    far = [cross(rotated[0])]
    inner_others = [over_band(part) for part in inner]
    for c in chunks[1:]:
        rotated += rotate(pieces, matrix, starts[c], [chunk], later=())[0]
        far.append(cross(rotated[c]))
    rotated_inner, _ = rotate(by_band(inner, inner_others), matrix, 0, [chunk for _ in chunks], later=far[1:])
    state = [[rotated[c], rotated_inner[c]] for c in chunks]
    beside = [[far[c], intra(rotated_inner[c])] for c in chunks]

    before = [nothing for _ in chunks]
    for _ in range(2):
        for c in chunks:
            new = apply_step(shared, (0, 1), state[c], beside[c], before[c])
            before[c], state[c] = state[c], new
            beside[c] = halos(new)
    out = None
    for c in chunks:
        for sides in ((0, 1),) if c < chunks[-1] else ((1,), (0,)):
            (out,) = apply_step(
                shared, sides, state[c], [beside[c][side] for side in sides], [before[c][side] for side in sides],
                out=out, out_column=starts[c], out_shape=start_bands.shape,
            )
    return out


def solution(mesh):
    return jax.shard_map(
        body,
        mesh=mesh,
        in_specs=(
            P("elem", None, "band"),
            P("elem", None, None, None),
            P("elem", None),
            P(),
            P("elem", "band"),
        ),
        out_specs=P("elem", None, "band"),
        check_vma=False,
    )
```

```python
import functools

import jax
import jax.numpy as jnp
from jax import lax
from jax.experimental import pallas as pl
from jax.experimental.pallas import tpu as pltpu
from jax.sharding import PartitionSpec as P

GY = 3
CHUNK = 256
MIB = 1024 * 1024
LONG, SHORT = 4 * 10**9, 10**8
PARAMS = pltpu.CompilerParams(vmem_limit_bytes=16 * MIB)
SMEM = pl.BlockSpec(memory_space=pltpu.SMEM)
VMEM = pl.BlockSpec(memory_space=pltpu.VMEM)
ANYWHERE = pl.BlockSpec(memory_space=pl.ANY)
HBM = pl.BlockSpec(memory_space=pltpu.HBM)


def cost(flops):
    return pl.CostEstimate(flops=flops, bytes_accessed=1024, transcendentals=0)


def like(array):
    return jax.ShapeDtypeStruct(array.shape, array.dtype)


def bands_of(count, basis, width):
    return jax.ShapeDtypeStruct((count, basis, width), jnp.bfloat16)


def first_row(side, odd):
    return odd * GY if side == 0 else (1 - odd) * GY


def run_copies(pairs, sems):
    copies = [pltpu.make_async_copy(source, target, sems.at[n]) for n, (source, target) in enumerate(pairs)]
    for copy in copies:
        copy.start()
    return copies


def split_kernel(starts, width, extra, passed, odd_ref, start_ref, *refs):
    targets, sems = refs[extra : len(refs) - passed - 1], refs[-1]
    pairs = []
    for n, target in enumerate(targets):
        rows = pl.ds(first_row(n % 2, odd_ref[0]), GY)
        pairs.append((start_ref.at[rows, :, pl.ds(starts[n // 2], width)], target))
    for copy in run_copies(pairs, sems):
        copy.wait()


def split(odd, start_bands, starts, width, passed, later):
    basis, count = start_bands.shape[1], 2 * len(starts)
    extra = len(passed) + len(later)
    result = pl.pallas_call(
        functools.partial(split_kernel, starts, width, extra, len(passed)),
        out_shape=[bands_of(GY, basis, width)] * count + [like(p) for p in passed],
        in_specs=[SMEM, HBM] + [ANYWHERE] * extra,
        out_specs=[VMEM] * count + [ANYWHERE] * len(passed),
        scratch_shapes=[pltpu.SemaphoreType.DMA((max(count, 1),))],
        input_output_aliases={2 + i: count + i for i in range(len(passed))},
        compiler_params=PARAMS,
        cost_estimate=cost(LONG),
    )(odd, start_bands, *passed, *later)
    return [[result[2 * n], result[2 * n + 1]] for n in range(len(starts))], list(result[count:])


def step_kernel(sides, firsts, out_column, has_out, waits, joined, odd_ref, links_ref, blocks_ref, *refs):
    refs = list(refs)

    def take(count):
        taken = refs[:count]
        del refs[:count]
        return taken

    current = take(2)
    halos = take(len(sides))
    before = [None if first else take(1)[0] for first in firsts]
    join = take(2 * joined)
    take(waits + has_out)
    results = take(1 if out_column is not None else len(sides))
    join_out = take(joined)
    if out_column is not None:
        made, left = take(2)
    copies = []
    if joined:
        rows = join[0].shape[0]
        copies = run_copies([(join[0], join_out[0].at[:rows]), (join[1], join_out[0].at[rows:])], refs[0])
    odd = odd_ref[0]
    for i, side in enumerate(sides):
        far_side = 1 + odd if side == 0 else 2 - odd
        near_side = 3 - far_side
        for k in range(GY):
            row = first_row(side, odd) + k

            def term(s, column):
                slot = lax.rem(links_ref[row, s], GY)
                return jnp.dot(blocks_ref[row, s], column[slot], preferred_element_type=jnp.float32)

            total = term(0, current[side])
            total += term(3, current[side])
            total += term(4, current[side])
            total += term(near_side, current[1 - side])
            total += term(far_side, halos[i])
            if before[i] is not None:
                total = 2.0 * total - before[i][k].astype(jnp.float32)
            if out_column is None:
                results[i][k] = total.astype(jnp.bfloat16)
            else:
                n = i * GY + k
                made[n] = total.astype(jnp.bfloat16)
                place = results[0].at[row, :, pl.ds(out_column, made.shape[2])]
                copy = pltpu.make_async_copy(made.at[n], place, left.at[n])
                copy.start()
                copies.append(copy)
    for copy in copies:
        copy.wait()


def apply_step(shared, sides, current, halos, before, out=None, out_column=None, out_shape=None, later=(), join=()):
    basis, width = current[0].shape[1:]
    operands = list(shared) + list(current) + list(halos) + [b for b in before if b is not None] + list(join)
    specs = [SMEM, SMEM] + [VMEM] * (len(operands) - 2) + [ANYWHERE] * len(later)
    operands += list(later)
    aliases, scratch = {}, []
    if out_column is None:
        shapes = [bands_of(GY, basis, width)] * len(sides)
        out_specs = [VMEM] * len(sides)
    else:
        if out is not None:
            aliases = {len(operands): 0}
            operands.append(out)
            specs.append(ANYWHERE)
        shapes, out_specs = [jax.ShapeDtypeStruct(out_shape, jnp.bfloat16)], [ANYWHERE]
        parts = len(sides) * GY
        scratch = [pltpu.VMEM((parts, basis, width), jnp.bfloat16), pltpu.SemaphoreType.DMA((parts,))]
    if join:
        rows = join[0].shape[0] + join[1].shape[0]
        shapes.append(jax.ShapeDtypeStruct((rows,) + join[0].shape[1:], join[0].dtype))
        out_specs.append(VMEM)
        scratch.append(pltpu.SemaphoreType.DMA((2,)))
    firsts = [b is None for b in before]
    return pl.pallas_call(
        functools.partial(step_kernel, sides, firsts, out_column, out is not None, len(later), int(bool(join))),
        out_shape=shapes,
        in_specs=specs,
        out_specs=out_specs,
        scratch_shapes=scratch,
        input_output_aliases=aliases,
        compiler_params=PARAMS,
        cost_estimate=cost(LONG),
    )(*operands)


def rotate_kernel(count, column, extra, passed, *refs):
    pieces, matrix = refs[:count], refs[count]
    outs = refs[count + 1 + extra : len(refs) - passed]
    for k in range(GY):
        rows = jnp.concatenate([piece[k] for piece in pieces], axis=1)
        start = column
        for out in outs:
            width = out.shape[2]
            out[k] = jnp.dot(
                rows, matrix[:, start : start + width], preferred_element_type=jnp.float32
            ).astype(jnp.bfloat16)
            start += width


def rotate(pieces, matrix, column, widths, passed=(), later=()):
    basis = pieces[0].shape[1]
    count = len(pieces) + 1
    result = pl.pallas_call(
        functools.partial(rotate_kernel, len(pieces), column, len(passed) + len(later), len(passed)),
        out_shape=[bands_of(GY, basis, width) for width in widths] + [like(p) for p in passed],
        in_specs=[VMEM] * count + [ANYWHERE] * (len(passed) + len(later)),
        out_specs=[VMEM] * len(widths) + [ANYWHERE] * len(passed),
        input_output_aliases={count + i: len(widths) + i for i in range(len(passed))},
        compiler_params=PARAMS,
        cost_estimate=cost(SHORT),
    )(*pieces, matrix, *passed, *later)
    return list(result[: len(widths)]), list(result[len(widths) :])


def wait_kernel(*refs):
    del refs


def after(arrays, later, weight=LONG):
    count = len(arrays)
    return pl.pallas_call(
        wait_kernel,
        out_shape=[like(array) for array in arrays],
        in_specs=[ANYWHERE] * (count + len(later)),
        out_specs=[ANYWHERE] * count,
        input_output_aliases={i: i for i in range(count)},
        compiler_params=PARAMS,
        cost_estimate=cost(weight),
    )(*arrays, *later)


def ordered_kernel(bands, count, own_ref, order_ref, *refs):
    rows, out_ref = refs[:count], refs[-1]
    total = out_ref.shape[0]
    width = total // bands
    for shift in range(bands):
        for start in range(0, width, 256):
            size = min(256, width - start)
            first = jnp.bitwise_xor(own_ref[0], shift) * width + start
            band = lax.broadcasted_iota(jnp.int32, (size, total), 0) + first
            choice = (band == order_ref[...]).astype(jnp.float32).astype(jnp.bfloat16)
            result, column = None, 0
            for part in rows:
                held = choice[:, column : column + part.shape[0]]
                found = jnp.dot(held, part[...], preferred_element_type=jnp.float32)
                result = found if result is None else result + found
                column += part.shape[0]
            place = shift * width + start
            out_ref[place : place + size, :] = result.astype(jnp.bfloat16)


def ordered_rows(own, order, rows, bands, later):
    total = order.shape[1]
    return pl.pallas_call(
        functools.partial(ordered_kernel, bands, len(rows)),
        out_shape=jax.ShapeDtypeStruct((total, rows[0].shape[1]), rows[0].dtype),
        in_specs=[SMEM] + [VMEM] * (1 + len(rows)) + [ANYWHERE] * len(later),
        out_specs=VMEM,
        compiler_params=PARAMS,
        cost_estimate=cost(LONG),
    )(own, order, *rows, *later)


def exchange(array, axis, partner):
    return lax.ppermute(array, axis, [(i, partner(i)) for i in range(lax.axis_size(axis))])


def bits_of(elems):
    bits = [1 << b for b in range(elems.bit_length() - 1)]
    return bits[1:2] + bits[:1:-1] + bits[:1]


def owners_of(elems):
    owners = [0]
    for bit in bits_of(elems):
        owners = owners + [owner ^ bit for owner in owners]
    return owners


class Gather:
    def __init__(self, rows):
        self.bits = bits_of(lax.axis_size("elem"))
        self.held = rows
        self.received = self.send()

    def send(self):
        bit = self.bits.pop(0)
        return exchange(self.held, "elem", lambda i: i ^ bit)

    def parts(self):
        return [self.held, self.received]

    def step(self, *args, **kwargs):
        if len(self.bits) < 2:
            return apply_step(*args, **kwargs)
        result = apply_step(*args, join=self.parts(), **kwargs)
        self.held = result[-1]
        self.received = self.send()
        return result[:-1]

    def finish(self):
        while len(self.bits) > 1:
            self.held = jnp.concatenate(self.parts(), axis=0)
            self.received = self.send()
        parts = self.parts()
        for bit in self.bits:
            parts = parts + [exchange(part, "elem", lambda i: i ^ bit) for part in parts]
            return parts


def body(start_bands, blocks, neighbours, band_order, rotation):
    elem_count, basis, width = start_bands.shape
    assert elem_count == 2 * GY
    elems, bands = lax.axis_size("elem"), lax.axis_size("band")
    me = lax.axis_index("elem")
    odd = (me % 2).astype(jnp.int32).reshape(1)
    chunk = min(CHUNK, width)
    starts = list(range(0, width, chunk))
    chunks = range(len(starts))
    nothing = [None, None]

    def cross(array):
        return exchange(array, "elem", lambda i: (i - 1) % elems if i % 2 == 0 else (i + 1) % elems)

    def intra(array):
        return exchange(array, "elem", lambda i: i ^ 1)

    def halos(columns):
        return [cross(columns[0]), intra(columns[1])]

    def over_band(piece):
        return [exchange(piece, "band", lambda i: i ^ shift) for shift in range(1, bands)]

    place = (me % 2) * GY
    state = [
        [
            lax.dynamic_slice(start_bands, (first, 0, starts[0]), (GY, basis, chunk))
            for first in (place, GY - place)
        ]
    ]
    beside = [halos(state[0])]
    order = band_order.reshape(elems, -1)[jnp.bitwise_xor(me, jnp.array(owners_of(elems)))].reshape(1, -1)
    rest, (order,) = split(odd, start_bands, starts[1:], chunk, [order], later=beside[0][1:])
    state += rest
    beside += [halos(columns) for columns in rest]
    shared = (odd, neighbours, blocks)
    gather = Gather(rotation)

    before = [nothing for _ in chunks]
    for n in range(2):
        for c in chunks:
            step = gather.step if (n, c) in ((0, 0), (1, chunks[-1])) else apply_step
            new = step(shared, (0, 1), state[c], beside[c], before[c], later=state[c - 1][:1] if c or before[0][0] is not None else ())
            before[c], state[c] = state[c], new
            beside[c] = halos(new)

    inner, outer, outer_others = [], [], []
    for c in chunks:
        made = apply_step(shared, (0, 1), state[c], beside[c], before[c], later=state[c - 1][:1] if c == 0 else outer[-1:])
        outer.append(made[0])
        inner.append(made[1])
        outer_others.append(over_band(made[0]))
    rows = gather.finish()
    inner = after(inner, outer_others[0])
    inner = after(inner, outer_others[-1], SHORT)
    inner_others = [over_band(part) for part in inner]
    matrix = ordered_rows(lax.axis_index("band").astype(jnp.int32).reshape(1), order, rows, bands, later=outer_others[-1] + list(inner[:1]))

    def by_band(own, others):
        return list(own) + [other[shift] for shift in range(bands - 1) for other in others]

    pieces = by_band(outer, outer_others)
    rotated, _ = rotate(pieces, matrix, 0, [chunk])
    far = [cross(rotated[0])]
    for c in chunks[1:]:
        rotated += rotate(pieces, matrix, starts[c], [chunk], later=())[0]
        far.append(cross(rotated[c]))
    if bands > 1:
        arrived = list(after([p for others in inner_others for p in others], []))
        inner_others = [arrived[n * (bands - 1) : (n + 1) * (bands - 1)] for n in range(len(chunks))]
    rotated_inner, _ = rotate(by_band(inner, inner_others), matrix, 0, [chunk for _ in chunks], later=far[1:])
    state = [[rotated[c], rotated_inner[c]] for c in chunks]
    beside = [[far[c], intra(rotated_inner[c])] for c in chunks]

    before = [nothing for _ in chunks]
    for _ in range(2):
        for c in chunks:
            new = apply_step(shared, (0, 1), state[c], beside[c], before[c])
            before[c], state[c] = state[c], new
            beside[c] = halos(new)
    out = None
    for c in chunks:
        for sides in ((0, 1),) if c < chunks[-1] else ((1,), (0,)):
            (out,) = apply_step(
                shared, sides, state[c], [beside[c][side] for side in sides], [before[c][side] for side in sides],
                out=out, out_column=starts[c], out_shape=start_bands.shape,
            )
    return out


def solution(mesh):
    return jax.shard_map(
        body,
        mesh=mesh,
        in_specs=(
            P("elem", None, "band"),
            P("elem", None, None, None),
            P("elem", None),
            P(),
            P("elem", "band"),
        ),
        out_specs=P("elem", None, "band"),
        check_vma=False,
    )
```

```python
import functools

import jax
import jax.numpy as jnp
from jax import lax
from jax.experimental import pallas as pl
from jax.experimental.pallas import tpu as pltpu
from jax.sharding import PartitionSpec as P

GY = 3
CHUNK = 256
MIB = 1024 * 1024
LONG, SHORT = 4 * 10**9, 10**8
PARAMS = pltpu.CompilerParams(vmem_limit_bytes=16 * MIB)
SMEM = pl.BlockSpec(memory_space=pltpu.SMEM)
VMEM = pl.BlockSpec(memory_space=pltpu.VMEM)
ANYWHERE = pl.BlockSpec(memory_space=pl.ANY)
HBM = pl.BlockSpec(memory_space=pltpu.HBM)


def cost(flops):
    return pl.CostEstimate(flops=flops, bytes_accessed=1024, transcendentals=0)


def like(array):
    return jax.ShapeDtypeStruct(array.shape, array.dtype)


def bands_of(count, basis, width):
    return jax.ShapeDtypeStruct((count, basis, width), jnp.bfloat16)


def first_row(side, odd):
    return odd * GY if side == 0 else (1 - odd) * GY


def run_copies(pairs, sems):
    copies = [pltpu.make_async_copy(source, target, sems.at[n]) for n, (source, target) in enumerate(pairs)]
    for copy in copies:
        copy.start()
    return copies


def split_kernel(starts, width, extra, passed, odd_ref, start_ref, *refs):
    targets, sems = refs[extra : len(refs) - passed - 1], refs[-1]
    pairs = []
    for n, target in enumerate(targets):
        rows = pl.ds(first_row(n % 2, odd_ref[0]), GY)
        pairs.append((start_ref.at[rows, :, pl.ds(starts[n // 2], width)], target))
    for copy in run_copies(pairs, sems):
        copy.wait()


def split(odd, start_bands, starts, width, passed, later):
    basis, count = start_bands.shape[1], 2 * len(starts)
    extra = len(passed) + len(later)
    result = pl.pallas_call(
        functools.partial(split_kernel, starts, width, extra, len(passed)),
        out_shape=[bands_of(GY, basis, width)] * count + [like(p) for p in passed],
        in_specs=[SMEM, HBM] + [ANYWHERE] * extra,
        out_specs=[VMEM] * count + [ANYWHERE] * len(passed),
        scratch_shapes=[pltpu.SemaphoreType.DMA((max(count, 1),))],
        input_output_aliases={2 + i: count + i for i in range(len(passed))},
        compiler_params=PARAMS,
        cost_estimate=cost(LONG),
    )(odd, start_bands, *passed, *later)
    return [[result[2 * n], result[2 * n + 1]] for n in range(len(starts))], list(result[count:])


def step_kernel(sides, firsts, out_column, has_out, waits, joined, odd_ref, links_ref, blocks_ref, *refs):
    refs = list(refs)

    def take(count):
        taken = refs[:count]
        del refs[:count]
        return taken

    current = take(2)
    halos = take(len(sides))
    before = [None if first else take(1)[0] for first in firsts]
    join = take(2 * joined)
    take(waits + has_out)
    results = take(1 if out_column is not None else len(sides))
    join_out = take(joined)
    if out_column is not None:
        made, left = take(2)
    copies = []
    if joined:
        rows = join[0].shape[0]
        copies = run_copies([(join[0], join_out[0].at[:rows]), (join[1], join_out[0].at[rows:])], refs[0])
    odd = odd_ref[0]
    for i, side in enumerate(sides):
        far_side = 1 + odd if side == 0 else 2 - odd
        near_side = 3 - far_side
        for k in range(GY):
            row = first_row(side, odd) + k

            def term(s, column):
                slot = lax.rem(links_ref[row, s], GY)
                return jnp.dot(blocks_ref[row, s], column[slot], preferred_element_type=jnp.float32)

            total = term(0, current[side])
            total += term(3, current[side])
            total += term(4, current[side])
            total += term(near_side, current[1 - side])
            total += term(far_side, halos[i])
            if before[i] is not None:
                total = 2.0 * total - before[i][k].astype(jnp.float32)
            if out_column is None:
                results[i][k] = total.astype(jnp.bfloat16)
            else:
                n = i * GY + k
                made[n] = total.astype(jnp.bfloat16)
                place = results[0].at[row, :, pl.ds(out_column, made.shape[2])]
                copy = pltpu.make_async_copy(made.at[n], place, left.at[n])
                copy.start()
                copies.append(copy)
    for copy in copies:
        copy.wait()


def apply_step(shared, sides, current, halos, before, out=None, out_column=None, out_shape=None, later=(), join=()):
    basis, width = current[0].shape[1:]
    operands = list(shared) + list(current) + list(halos) + [b for b in before if b is not None] + list(join)
    specs = [SMEM, SMEM] + [VMEM] * (len(operands) - 2) + [ANYWHERE] * len(later)
    operands += list(later)
    aliases, scratch = {}, []
    if out_column is None:
        shapes = [bands_of(GY, basis, width)] * len(sides)
        out_specs = [VMEM] * len(sides)
    else:
        if out is not None:
            aliases = {len(operands): 0}
            operands.append(out)
            specs.append(ANYWHERE)
        shapes, out_specs = [jax.ShapeDtypeStruct(out_shape, jnp.bfloat16)], [ANYWHERE]
        parts = len(sides) * GY
        scratch = [pltpu.VMEM((parts, basis, width), jnp.bfloat16), pltpu.SemaphoreType.DMA((parts,))]
    if join:
        rows = join[0].shape[0] + join[1].shape[0]
        shapes.append(jax.ShapeDtypeStruct((rows,) + join[0].shape[1:], join[0].dtype))
        out_specs.append(VMEM)
        scratch.append(pltpu.SemaphoreType.DMA((2,)))
    firsts = [b is None for b in before]
    return pl.pallas_call(
        functools.partial(step_kernel, sides, firsts, out_column, out is not None, len(later), int(bool(join))),
        out_shape=shapes,
        in_specs=specs,
        out_specs=out_specs,
        scratch_shapes=scratch,
        input_output_aliases=aliases,
        compiler_params=PARAMS,
        cost_estimate=cost(LONG),
    )(*operands)


def rotate_kernel(count, column, extra, passed, *refs):
    pieces, matrix = refs[:count], refs[count]
    outs = refs[count + 1 + extra : len(refs) - passed]
    for k in range(GY):
        rows = jnp.concatenate([piece[k] for piece in pieces], axis=1)
        start = column
        for out in outs:
            width = out.shape[2]
            out[k] = jnp.dot(
                rows, matrix[:, start : start + width], preferred_element_type=jnp.float32
            ).astype(jnp.bfloat16)
            start += width


def rotate(pieces, matrix, column, widths, passed=(), later=()):
    basis = pieces[0].shape[1]
    count = len(pieces) + 1
    result = pl.pallas_call(
        functools.partial(rotate_kernel, len(pieces), column, len(passed) + len(later), len(passed)),
        out_shape=[bands_of(GY, basis, width) for width in widths] + [like(p) for p in passed],
        in_specs=[VMEM] * count + [ANYWHERE] * (len(passed) + len(later)),
        out_specs=[VMEM] * len(widths) + [ANYWHERE] * len(passed),
        input_output_aliases={count + i: len(widths) + i for i in range(len(passed))},
        compiler_params=PARAMS,
        cost_estimate=cost(SHORT),
    )(*pieces, matrix, *passed, *later)
    return list(result[: len(widths)]), list(result[len(widths) :])


def wait_kernel(*refs):
    del refs


def after(arrays, later, weight=LONG):
    count = len(arrays)
    return pl.pallas_call(
        wait_kernel,
        out_shape=[like(array) for array in arrays],
        in_specs=[ANYWHERE] * (count + len(later)),
        out_specs=[ANYWHERE] * count,
        input_output_aliases={i: i for i in range(count)},
        compiler_params=PARAMS,
        cost_estimate=cost(weight),
    )(*arrays, *later)


def ordered_kernel(bands, count, own_ref, order_ref, *refs):
    rows, out_ref = refs[:count], refs[-1]
    total = out_ref.shape[0]
    width = total // bands
    for shift in range(bands):
        for start in range(0, width, 256):
            size = min(256, width - start)
            first = jnp.bitwise_xor(own_ref[0], shift) * width + start
            band = lax.broadcasted_iota(jnp.int32, (size, total), 0) + first
            choice = (band == order_ref[...]).astype(jnp.float32).astype(jnp.bfloat16)
            result, column = None, 0
            for part in rows:
                held = choice[:, column : column + part.shape[0]]
                found = jnp.dot(held, part[...], preferred_element_type=jnp.float32)
                result = found if result is None else result + found
                column += part.shape[0]
            place = shift * width + start
            out_ref[place : place + size, :] = result.astype(jnp.bfloat16)


def ordered_rows(own, order, rows, bands, later):
    total = order.shape[1]
    return pl.pallas_call(
        functools.partial(ordered_kernel, bands, len(rows)),
        out_shape=jax.ShapeDtypeStruct((total, rows[0].shape[1]), rows[0].dtype),
        in_specs=[SMEM] + [VMEM] * (1 + len(rows)) + [ANYWHERE] * len(later),
        out_specs=VMEM,
        compiler_params=PARAMS,
        cost_estimate=cost(LONG),
    )(own, order, *rows, *later)


def exchange(array, axis, partner):
    return lax.ppermute(array, axis, [(i, partner(i)) for i in range(lax.axis_size(axis))])


def bits_of(elems):
    bits = [1 << b for b in range(elems.bit_length() - 1)]
    return bits[1:2] + bits[2:] + bits[:1]


def owners_of(elems):
    owners = [0]
    for bit in bits_of(elems):
        owners = owners + [owner ^ bit for owner in owners]
    return owners


class Gather:
    def __init__(self, rows):
        self.bits = bits_of(lax.axis_size("elem"))
        self.held = rows
        self.received = self.send()

    def send(self):
        bit = self.bits.pop(0)
        return exchange(self.held, "elem", lambda i: i ^ bit)

    def parts(self):
        return [self.held, self.received]

    def step(self, *args, **kwargs):
        if len(self.bits) < 2:
            return apply_step(*args, **kwargs)
        result = apply_step(*args, join=self.parts(), **kwargs)
        self.held = result[-1]
        self.received = self.send()
        return result[:-1]

    def finish(self):
        while len(self.bits) > 1:
            self.held = jnp.concatenate(self.parts(), axis=0)
            self.received = self.send()
        parts = self.parts()
        for bit in self.bits:
            parts = parts + [exchange(part, "elem", lambda i: i ^ bit) for part in parts]
            return parts


def body(start_bands, blocks, neighbours, band_order, rotation):
    elem_count, basis, width = start_bands.shape
    assert elem_count == 2 * GY
    elems, bands = lax.axis_size("elem"), lax.axis_size("band")
    me = lax.axis_index("elem")
    odd = (me % 2).astype(jnp.int32).reshape(1)
    chunk = min(CHUNK, width)
    starts = list(range(0, width, chunk))
    chunks = range(len(starts))
    nothing = [None, None]

    def cross(array):
        return exchange(array, "elem", lambda i: (i - 1) % elems if i % 2 == 0 else (i + 1) % elems)

    def intra(array):
        return exchange(array, "elem", lambda i: i ^ 1)

    def halos(columns):
        return [cross(columns[0]), intra(columns[1])]

    def over_band(piece):
        return [exchange(piece, "band", lambda i: i ^ shift) for shift in range(1, bands)]

    place = (me % 2) * GY
    state = [
        [
            lax.dynamic_slice(start_bands, (first, 0, starts[0]), (GY, basis, chunk))
            for first in (place, GY - place)
        ]
    ]
    beside = [halos(state[0])]
    order = band_order.reshape(elems, -1)[jnp.bitwise_xor(me, jnp.array(owners_of(elems)))].reshape(1, -1)
    rest, (order,) = split(odd, start_bands, starts[1:], chunk, [order], later=beside[0][1:])
    state += rest
    beside += [halos(columns) for columns in rest]
    shared = (odd, neighbours, blocks)
    gather = Gather(rotation)

    before = [nothing for _ in chunks]
    for n in range(2):
        for c in chunks:
            step = gather.step if (n, c) in ((0, 0), (1, chunks[-1])) else apply_step
            new = step(shared, (0, 1), state[c], beside[c], before[c], later=state[c - 1][:1] if c or before[0][0] is not None else ())
            before[c], state[c] = state[c], new
            beside[c] = halos(new)

    inner, outer, outer_others = [], [], []
    for c in chunks:
        made = apply_step(shared, (0, 1), state[c], beside[c], before[c], later=state[c - 1][:1] if c == 0 else outer[-1:])
        outer.append(made[0])
        inner.append(made[1])
        outer_others.append(over_band(made[0]))
    rows = gather.finish()
    inner = after(inner, outer_others[0])
    inner = after(inner, outer_others[-1], SHORT)
    inner_others = [over_band(part) for part in inner]
    matrix = ordered_rows(lax.axis_index("band").astype(jnp.int32).reshape(1), order, rows, bands, later=outer_others[-1] + list(inner[:1]))

    def by_band(own, others):
        return list(own) + [other[shift] for shift in range(bands - 1) for other in others]

    pieces = by_band(outer, outer_others)
    rotated, _ = rotate(pieces, matrix, 0, [chunk])
    far = [cross(rotated[0])]
    for c in chunks[1:]:
        rotated += rotate(pieces, matrix, starts[c], [chunk], later=())[0]
        far.append(cross(rotated[c]))
    if bands > 1:
        arrived = list(after([p for others in inner_others for p in others], []))
        inner_others = [arrived[n * (bands - 1) : (n + 1) * (bands - 1)] for n in range(len(chunks))]
    rotated_inner, _ = rotate(by_band(inner, inner_others), matrix, 0, [chunk for _ in chunks], later=far[:1])
    state = [[rotated[c], rotated_inner[c]] for c in chunks]
    beside = [[far[c], intra(rotated_inner[c])] for c in chunks]

    before = [nothing for _ in chunks]
    backwards = chunks[::-1]
    for _ in range(2):
        for c in backwards:
            new = apply_step(shared, (0, 1), state[c], beside[c], before[c])
            before[c], state[c] = state[c], new
            beside[c] = halos(new)
    out = None
    for c in backwards:
        for sides in ((0, 1),) if c != backwards[-1] else ((1,), (0,)):
            (out,) = apply_step(
                shared, sides, state[c], [beside[c][side] for side in sides], [before[c][side] for side in sides],
                out=out, out_column=starts[c], out_shape=start_bands.shape,
            )
    return out


def solution(mesh):
    return jax.shard_map(
        body,
        mesh=mesh,
        in_specs=(
            P("elem", None, "band"),
            P("elem", None, None, None),
            P("elem", None),
            P(),
            P("elem", "band"),
        ),
        out_specs=P("elem", None, "band"),
        check_vma=False,
    )
```

```python
import functools

import jax
import jax.numpy as jnp
from jax import lax
from jax.experimental import pallas as pl
from jax.experimental.pallas import tpu as pltpu
from jax.sharding import PartitionSpec as P

GY = 3
CHUNK = 256
MIB = 1024 * 1024
LONG, SHORT = 4 * 10**9, 10**8
PARAMS = pltpu.CompilerParams(vmem_limit_bytes=16 * MIB)
SMEM = pl.BlockSpec(memory_space=pltpu.SMEM)
VMEM = pl.BlockSpec(memory_space=pltpu.VMEM)
ANYWHERE = pl.BlockSpec(memory_space=pl.ANY)
HBM = pl.BlockSpec(memory_space=pltpu.HBM)


def cost(flops):
    return pl.CostEstimate(flops=flops, bytes_accessed=1024, transcendentals=0)


def like(array):
    return jax.ShapeDtypeStruct(array.shape, array.dtype)


def bands_of(count, basis, width):
    return jax.ShapeDtypeStruct((count, basis, width), jnp.bfloat16)


def first_row(side, odd):
    return odd * GY if side == 0 else (1 - odd) * GY


def run_copies(pairs, sems):
    copies = [pltpu.make_async_copy(source, target, sems.at[n]) for n, (source, target) in enumerate(pairs)]
    for copy in copies:
        copy.start()
    return copies


def split_kernel(starts, width, extra, passed, odd_ref, start_ref, *refs):
    targets, sems = refs[extra : len(refs) - passed - 1], refs[-1]
    pairs = []
    for n, target in enumerate(targets):
        rows = pl.ds(first_row(n % 2, odd_ref[0]), GY)
        pairs.append((start_ref.at[rows, :, pl.ds(starts[n // 2], width)], target))
    for copy in run_copies(pairs, sems):
        copy.wait()


def split(odd, start_bands, starts, width, passed, later):
    basis, count = start_bands.shape[1], 2 * len(starts)
    extra = len(passed) + len(later)
    result = pl.pallas_call(
        functools.partial(split_kernel, starts, width, extra, len(passed)),
        out_shape=[bands_of(GY, basis, width)] * count + [like(p) for p in passed],
        in_specs=[SMEM, HBM] + [ANYWHERE] * extra,
        out_specs=[VMEM] * count + [ANYWHERE] * len(passed),
        scratch_shapes=[pltpu.SemaphoreType.DMA((max(count, 1),))],
        input_output_aliases={2 + i: count + i for i in range(len(passed))},
        compiler_params=PARAMS,
        cost_estimate=cost(LONG),
    )(odd, start_bands, *passed, *later)
    return [[result[2 * n], result[2 * n + 1]] for n in range(len(starts))], list(result[count:])


def step_kernel(sides, firsts, out_column, has_out, waits, joined, odd_ref, links_ref, blocks_ref, *refs):
    refs = list(refs)

    def take(count):
        taken = refs[:count]
        del refs[:count]
        return taken

    current = take(2)
    halos = take(len(sides))
    before = [None if first else take(1)[0] for first in firsts]
    join = take(2 * joined)
    take(waits + has_out)
    results = take(1 if out_column is not None else len(sides))
    join_out = take(joined)
    if out_column is not None:
        made, left = take(2)
    copies = []
    if joined:
        rows = join[0].shape[0]
        copies = run_copies([(join[0], join_out[0].at[:rows]), (join[1], join_out[0].at[rows:])], refs[0])
    odd = odd_ref[0]
    for i, side in enumerate(sides):
        far_side = 1 + odd if side == 0 else 2 - odd
        near_side = 3 - far_side
        for k in range(GY):
            row = first_row(side, odd) + k

            def term(s, column):
                slot = lax.rem(links_ref[row, s], GY)
                return jnp.dot(blocks_ref[row, s], column[slot], preferred_element_type=jnp.float32)

            total = term(0, current[side])
            total += term(3, current[side])
            total += term(4, current[side])
            total += term(near_side, current[1 - side])
            total += term(far_side, halos[i])
            if before[i] is not None:
                total = 2.0 * total - before[i][k].astype(jnp.float32)
            if out_column is None:
                results[i][k] = total.astype(jnp.bfloat16)
            else:
                n = i * GY + k
                made[n] = total.astype(jnp.bfloat16)
                place = results[0].at[row, :, pl.ds(out_column, made.shape[2])]
                copy = pltpu.make_async_copy(made.at[n], place, left.at[n])
                copy.start()
                copies.append(copy)
    for copy in copies:
        copy.wait()


def apply_step(shared, sides, current, halos, before, out=None, out_column=None, out_shape=None, later=(), join=()):
    basis, width = current[0].shape[1:]
    operands = list(shared) + list(current) + list(halos) + [b for b in before if b is not None] + list(join)
    specs = [SMEM, SMEM] + [VMEM] * (len(operands) - 2) + [ANYWHERE] * len(later)
    operands += list(later)
    aliases, scratch = {}, []
    if out_column is None:
        shapes = [bands_of(GY, basis, width)] * len(sides)
        out_specs = [VMEM] * len(sides)
    else:
        if out is not None:
            aliases = {len(operands): 0}
            operands.append(out)
            specs.append(ANYWHERE)
        shapes, out_specs = [jax.ShapeDtypeStruct(out_shape, jnp.bfloat16)], [ANYWHERE]
        parts = len(sides) * GY
        scratch = [pltpu.VMEM((parts, basis, width), jnp.bfloat16), pltpu.SemaphoreType.DMA((parts,))]
    if join:
        rows = join[0].shape[0] + join[1].shape[0]
        shapes.append(jax.ShapeDtypeStruct((rows,) + join[0].shape[1:], join[0].dtype))
        out_specs.append(VMEM)
        scratch.append(pltpu.SemaphoreType.DMA((2,)))
    firsts = [b is None for b in before]
    return pl.pallas_call(
        functools.partial(step_kernel, sides, firsts, out_column, out is not None, len(later), int(bool(join))),
        out_shape=shapes,
        in_specs=specs,
        out_specs=out_specs,
        scratch_shapes=scratch,
        input_output_aliases=aliases,
        compiler_params=PARAMS,
        cost_estimate=cost(LONG),
    )(*operands)


def rotate_kernel(count, column, extra, passed, *refs):
    pieces, matrix = refs[:count], refs[count]
    outs = refs[count + 1 + extra : len(refs) - passed]
    for k in range(GY):
        rows = jnp.concatenate([piece[k] for piece in pieces], axis=1)
        start = column
        for out in outs:
            width = out.shape[2]
            out[k] = jnp.dot(
                rows, matrix[:, start : start + width], preferred_element_type=jnp.float32
            ).astype(jnp.bfloat16)
            start += width


def rotate(pieces, matrix, column, widths, passed=(), later=()):
    basis = pieces[0].shape[1]
    count = len(pieces) + 1
    result = pl.pallas_call(
        functools.partial(rotate_kernel, len(pieces), column, len(passed) + len(later), len(passed)),
        out_shape=[bands_of(GY, basis, width) for width in widths] + [like(p) for p in passed],
        in_specs=[VMEM] * count + [ANYWHERE] * (len(passed) + len(later)),
        out_specs=[VMEM] * len(widths) + [ANYWHERE] * len(passed),
        input_output_aliases={count + i: len(widths) + i for i in range(len(passed))},
        compiler_params=PARAMS,
        cost_estimate=cost(SHORT),
    )(*pieces, matrix, *passed, *later)
    return list(result[: len(widths)]), list(result[len(widths) :])


def wait_kernel(*refs):
    del refs


def after(arrays, later, weight=LONG):
    count = len(arrays)
    return pl.pallas_call(
        wait_kernel,
        out_shape=[like(array) for array in arrays],
        in_specs=[ANYWHERE] * (count + len(later)),
        out_specs=[ANYWHERE] * count,
        input_output_aliases={i: i for i in range(count)},
        compiler_params=PARAMS,
        cost_estimate=cost(weight),
    )(*arrays, *later)


def ordered_kernel(bands, count, own_ref, order_ref, *refs):
    rows, out_ref = refs[:count], refs[-1]
    total = out_ref.shape[0]
    width = total // bands
    for shift in range(bands):
        for start in range(0, width, 256):
            size = min(256, width - start)
            first = jnp.bitwise_xor(own_ref[0], shift) * width + start
            band = lax.broadcasted_iota(jnp.int32, (size, total), 0) + first
            choice = (band == order_ref[...]).astype(jnp.float32).astype(jnp.bfloat16)
            result, column = None, 0
            for part in rows:
                held = choice[:, column : column + part.shape[0]]
                found = jnp.dot(held, part[...], preferred_element_type=jnp.float32)
                result = found if result is None else result + found
                column += part.shape[0]
            place = shift * width + start
            out_ref[place : place + size, :] = result.astype(jnp.bfloat16)


def ordered_rows(own, order, rows, bands, later):
    total = order.shape[1]
    return pl.pallas_call(
        functools.partial(ordered_kernel, bands, len(rows)),
        out_shape=jax.ShapeDtypeStruct((total, rows[0].shape[1]), rows[0].dtype),
        in_specs=[SMEM] + [VMEM] * (1 + len(rows)) + [ANYWHERE] * len(later),
        out_specs=VMEM,
        compiler_params=PARAMS,
        cost_estimate=cost(LONG),
    )(own, order, *rows, *later)


def exchange(array, axis, partner):
    return lax.ppermute(array, axis, [(i, partner(i)) for i in range(lax.axis_size(axis))])


def bits_of(elems):
    bits = [1 << b for b in range(elems.bit_length() - 1)]
    return bits[1:2] + bits[2:] + bits[:1]


def owners_of(elems):
    owners = [0]
    for bit in bits_of(elems):
        owners = owners + [owner ^ bit for owner in owners]
    return owners


class Gather:
    def __init__(self, rows):
        self.bits = bits_of(lax.axis_size("elem"))
        self.held = rows
        self.received = self.send()

    def send(self):
        bit = self.bits.pop(0)
        return exchange(self.held, "elem", lambda i: i ^ bit)

    def parts(self):
        return [self.held, self.received]

    def step(self, *args, **kwargs):
        if len(self.bits) < 2:
            return apply_step(*args, **kwargs)
        result = apply_step(*args, join=self.parts(), **kwargs)
        self.held = result[-1]
        self.received = self.send()
        return result[:-1]

    def finish(self):
        while len(self.bits) > 1:
            self.held = jnp.concatenate(self.parts(), axis=0)
            self.received = self.send()
        parts = self.parts()
        for bit in self.bits:
            parts = parts + [exchange(part, "elem", lambda i: i ^ bit) for part in parts]
            return parts


def body(start_bands, blocks, neighbours, band_order, rotation):
    elem_count, basis, width = start_bands.shape
    assert elem_count == 2 * GY
    elems, bands = lax.axis_size("elem"), lax.axis_size("band")
    me = lax.axis_index("elem")
    odd = (me % 2).astype(jnp.int32).reshape(1)
    chunk = min(CHUNK, width)
    starts = list(range(0, width, chunk))
    chunks = range(len(starts))
    nothing = [None, None]

    def cross(array):
        return exchange(array, "elem", lambda i: (i - 1) % elems if i % 2 == 0 else (i + 1) % elems)

    def intra(array):
        return exchange(array, "elem", lambda i: i ^ 1)

    def halos(columns):
        return [cross(columns[0]), intra(columns[1])]

    def over_band(piece):
        return [exchange(piece, "band", lambda i: i ^ shift) for shift in range(1, bands)]

    place = (me % 2) * GY
    state = [
        [
            lax.dynamic_slice(start_bands, (first, 0, starts[0]), (GY, basis, chunk))
            for first in (place, GY - place)
        ]
    ]
    beside = [halos(state[0])]
    order = band_order.reshape(elems, -1)[jnp.bitwise_xor(me, jnp.array(owners_of(elems)))].reshape(1, -1)
    rest, (order,) = split(odd, start_bands, starts[1:], chunk, [order], later=beside[0][1:])
    state += rest
    beside += [halos(columns) for columns in rest]
    shared = (odd, neighbours, blocks)
    gather = Gather(rotation)

    before = [nothing for _ in chunks]
    for n in range(2):
        for c in chunks:
            step = gather.step if (n, c) in ((0, 0), (1, chunks[-1])) else apply_step
            new = step(shared, (0, 1), state[c], beside[c], before[c], later=state[c - 1][:1] if c or before[0][0] is not None else ())
            before[c], state[c] = state[c], new
            beside[c] = halos(new)

    inner, outer, outer_others = [], [], []
    for c in chunks:
        made = apply_step(shared, (0, 1), state[c], beside[c], before[c], later=state[c - 1][:1] if c == 0 else outer[-1:])
        outer.append(made[0])
        inner.append(made[1])
        outer_others.append(over_band(made[0]))
    rows = gather.finish()
    inner = after(inner, outer_others[0])
    inner = after(inner, outer_others[-1], SHORT)
    inner_others = [over_band(part) for part in inner]
    matrix = ordered_rows(lax.axis_index("band").astype(jnp.int32).reshape(1), order, rows, bands, later=outer_others[-1] + list(inner[:1]))

    def by_band(own, others):
        return list(own) + [other[shift] for shift in range(bands - 1) for other in others]

    pieces = by_band(outer, outer_others)
    rotated, _ = rotate(pieces, matrix, 0, [chunk])
    far = [cross(rotated[0])]
    for c in chunks[1:]:
        rotated += rotate(pieces, matrix, starts[c], [chunk], later=())[0]
        far.append(cross(rotated[c]))
    if bands > 1:
        arrived = list(after([p for others in inner_others for p in others], []))
        inner_others = [arrived[n * (bands - 1) : (n + 1) * (bands - 1)] for n in range(len(chunks))]
    rotated_inner, _ = rotate(by_band(inner, inner_others), matrix, 0, [chunk for _ in chunks], later=far[1:])
    state = [[rotated[c], rotated_inner[c]] for c in chunks]
    beside = [[far[c], intra(rotated_inner[c])] for c in chunks]

    before = [nothing for _ in chunks]
    for _ in range(2):
        for c in chunks:
            new = apply_step(shared, (0, 1), state[c], beside[c], before[c])
            before[c], state[c] = state[c], new
            beside[c] = halos(new)
    out = None
    for c in chunks:
        for sides in ((0, 1),) if c < chunks[-1] else ((1,), (0,)):
            (out,) = apply_step(
                shared, sides, state[c], [beside[c][side] for side in sides], [before[c][side] for side in sides],
                out=out, out_column=starts[c], out_shape=start_bands.shape,
            )
    return out


def solution(mesh):
    return jax.shard_map(
        body,
        mesh=mesh,
        in_specs=(
            P("elem", None, "band"),
            P("elem", None, None, None),
            P("elem", None),
            P(),
            P("elem", "band"),
        ),
        out_specs=P("elem", None, "band"),
        check_vma=False,
    )
```
